512 devices in a mesh: shard: 64 (over y, x, core), rep: 8 (over z).
Axes of the slice: x: 4, y: 8, z: 8, core: 2. Of those that a mesh axis runs over, the one named last changes fastest.
Arguments:
- pooled_grad: bfloat16 [65536, 64, 128], P(('shard', 'rep')), may hold values from -6 to 6
- cold_ids: int32 [65536, 64, 8], P(('shard', 'rep')), may hold values from 0 to 1023
- lengths: int32 [65536, 64], P(('shard', 'rep')), may hold values from 1 to 8
- hot_ids: int32 [65536, 64, 2], P(('shard', 'rep')), may hold values from 0 to 1023
- table: float32 [65536, 128], P('shard'), may hold values from -1.5 to 1.5
- accum: float32 [65536], P('shard'), may hold values from 100 to 1000
- hot_table: float32 [1024, 128], replicated, may hold values from -1.5 to 1.5
- hot_accum: float32 [1024], replicated, may hold values from 5000 to 50000
Outputs:
- new_table: float32 [65536, 128], P('shard')
- new_accum: float32 [65536], P('shard')
- new_hot_table: float32 [1024, 128], replicated
- new_hot_accum: float32 [1024], replicated
The draws below stay inside these ranges and needn't reach their ends.
All inputs are finite; a program needn't handle non-finite values.
Results may differ from the reference program's by a relative error of at most 0.0003.
Values may be sent and summed in bfloat16 or wider, within the bound.
No kernel may reach another device: no remote copies, remote signals or barrier semaphores. Data moves between devices by JAX's collectives and lax.ppermute only.
A program may use at most 64 MiB of HBM per device.

```python
import math
import jax
import jax.numpy as jnp
import numpy as np
from jax import lax

E = 128
V = 1024
H = 8
HH = 2
HOT = 1024
F = 64
BATCH = 65536
ROWS = 65536


def touch_ends(entries, stream_key, smallest, top_value):
    dims = entries.shape
    index_at = [jax.random.randint(jax.random.fold_in(stream_key, axis), (), 0, dims[axis]) for axis in range(len(dims))]
    entries = entries.at[tuple(index_at)].set(smallest)
    longest = dims.index(max(dims))
    index_at[longest] = (index_at[longest] + 1) % dims[longest]
    return entries.at[tuple(index_at)].set(top_value)


def steps_of(own_key, dims, split, least, largest):
    loudness = 1.0
    for dim, parts in split:
        heights = jax.random.uniform(jax.random.fold_in(jax.random.fold_in(own_key, 6), dim), (parts,), jnp.float32, least / len(split), largest / len(split))
        loudness = loudness * jnp.repeat(jnp.exp(heights), dims[dim] // parts).reshape((-1,) + (1,) * (len(dims) - 1 - dim))
    return loudness


def cumulative_ranks(count, lean):
    weights = [(1 << 20) // math.isqrt(rank ** lean) + 1 for rank in range(1, count + 1)]
    width = 1 + sum(weights) // (1 << 30)
    return np.cumsum(np.array([max(1, weight // width) for weight in weights]))


def ranked(rng, dims, number_of, lean):
    listing = cumulative_ranks(number_of, lean)
    ticket = jax.random.randint(jax.random.fold_in(rng, 1), dims, 0, int(listing[number_of - 1]))
    rank = jnp.searchsorted(jnp.asarray(listing, jnp.int32), ticket, side="right")
    return jax.random.permutation(jax.random.fold_in(rng, 2), number_of)[rank].astype(jnp.int32)


def bell_draw(own_key, dims, spread, reach, shards=(), kind=jnp.bfloat16):
    result = spread * jax.random.normal(own_key, dims, jnp.float32)
    if shards:
        result = result * steps_of(own_key, dims, shards, -0.22, 0.18)
    return jnp.clip(result, -reach, reach).astype(kind)


def setup_inputs(seed: int = 0) -> dict:
    arg_keys = jax.random.split(jax.random.key(seed), 9)
    return {
        "pooled_grad": bell_draw(arg_keys[0], (BATCH, F, E), 1.0, 6.0, ((0, 512),)),
        "cold_ids": touch_ends(ranked(arg_keys[1], (BATCH, F, H), V, 2), jax.random.fold_in(arg_keys[1], 3), 0, V - 1).astype(jnp.int32),
        "lengths": touch_ends(jax.random.randint(arg_keys[2], (BATCH, F), 1, H + 1), jax.random.fold_in(arg_keys[2], 1), 1, H).astype(jnp.int32),
        "hot_ids": touch_ends(jax.random.randint(arg_keys[3], (BATCH, F, HH), 0, HOT), jax.random.fold_in(arg_keys[3], 1), 0, HOT - 1).astype(jnp.int32),
        "table": bell_draw(arg_keys[4], (ROWS, E), 0.1, 1.5, ((0, 64),), jnp.float32),
        "accum": jnp.clip(jnp.exp(math.log(1000.0) - 2.3025851 * jax.random.uniform(arg_keys[5], (ROWS,), jnp.float32) ** steps_of(arg_keys[5], (ROWS,), ((0, 64),), -0.2, 0.2)), 100.0, 1000.0),
        "hot_table": bell_draw(arg_keys[6], (HOT, E), 0.1, 1.5, (), jnp.float32),
        "hot_accum": jnp.clip(jnp.exp(jax.random.uniform(arg_keys[7], (HOT,), jnp.float32, math.log(5000.0), math.log(50000.0))), 5000.0, 50000.0),
    }


learning_rate = 0.5
epsilon = 1e-06

def adagrad(weights, accumulator, grad):
    fresh = accumulator + lax.optimization_barrier(jnp.mean(grad * grad, axis=1))
    return (weights - learning_rate * grad / (jnp.sqrt(fresh)[:, None] + epsilon), fresh)

def reference(pooled_grad, cold_ids, lengths, hot_ids, table, accum, hot_table, hot_accum):
    position = lax.broadcasted_iota(jnp.int32, cold_ids.shape, 2)
    masked = jnp.where(position < lengths[:, :, None], cold_ids, V)
    features = jnp.arange(F, dtype=jnp.int32)

    def per_feature(carry, inputs):
        cold_grad, hot_grad = carry
        values, ids, hots, feature = inputs
        values = values.astype(jnp.float32)
        rows = jnp.where(ids < V, feature * V + ids, F * V).astype(jnp.int32)
        for slot in range(H):
            cold_grad = cold_grad.at[rows[:, slot]].add(values, mode='drop')
        for slot in range(HH):
            hot_grad = hot_grad.at[hots[:, slot]].add(values)
        return ((cold_grad, hot_grad), None)
    start = (jnp.zeros((F * V, E), jnp.float32), jnp.zeros((HOT, E), jnp.float32))
    (cold_grad, hot_grad), unused = lax.scan(per_feature, start, (jnp.moveaxis(pooled_grad, 1, 0), jnp.moveaxis(masked, 1, 0), jnp.moveaxis(hot_ids, 1, 0), features))
    new_table, new_accum = adagrad(table, accum, cold_grad)
    new_hot_table, new_hot_accum = adagrad(hot_table, hot_accum, hot_grad)
    return (new_table, new_accum, new_hot_table, new_hot_accum)
```

```python
import functools

import jax
import jax.numpy as jnp
from jax import lax
from jax.experimental import pallas as pl
from jax.experimental.pallas import tpu as pltpu
from jax.sharding import PartitionSpec as P

V = 1024
GROUP = 128
FIELDS = 8
BITS = 4

learning_rate = 0.5
epsilon = 1e-06


def adagrad(weights, accumulator, grad):
    fresh = accumulator + jnp.mean(grad * grad, axis=1)
    return (weights - learning_rate * grad / (jnp.sqrt(fresh)[:, None] + epsilon), fresh)


def encode_ids(cold_ids, lengths):
    ids = jnp.transpose(cold_ids, (1, 2, 0))
    used = jnp.transpose(lengths, (1, 0))[:, None, :]
    position = lax.broadcasted_iota(jnp.int32, ids.shape, 1)
    low, high = ids & (GROUP - 1), ids >> 7
    return jnp.where(position < used, (GROUP + low) << high, 0).astype(jnp.bfloat16)


def decode_ids(code):
    key = jnp.zeros(code.shape, jnp.float32)
    unit = jnp.zeros(code.shape, jnp.int32)
    for field in range(FIELDS):
        reached = code >= float(GROUP * 2**field)
        key = jnp.where(reached, code * 2.0**-field - float(GROUP), key)
        unit = jnp.where(reached, 1 << (BITS * field), unit)
    return key.astype(jnp.int32), unit


def packed_counts(key, unit):
    rows = lax.broadcasted_iota(jnp.int32, (GROUP, key.shape[1]), 0)
    total = jnp.where(rows == key[0:1], unit[0:1], 0)
    for slot in range(1, key.shape[0]):
        total = total + jnp.where(rows == key[slot : slot + 1], unit[slot : slot + 1], 0)
    return total


def unpacked_counts(packed):
    groups = []
    for field in range(FIELDS):
        if field == FIELDS - 1:
            part = lax.shift_right_logical(packed, jnp.int32(BITS * field))
        else:
            part = packed & jnp.int32(((1 << BITS) - 1) << (BITS * field))
        groups.append(part.astype(jnp.float32).astype(jnp.bfloat16))
    return jnp.concatenate(groups, 0)


def block_sum(bags, values, pair):
    total = None
    for first in range(0, len(bags), pair):
        counts = jnp.concatenate([unpacked_counts(packed_counts(*bag)) for bag in bags[first : first + pair]], 1)
        rows = jnp.concatenate(values[first : first + pair], 0)
        product = jnp.dot(counts, rows, preferred_element_type=jnp.float32)
        total = product if total is None else total + product
    return total


def hot_kernel(x_ref, ids_ref, out_ref, *, blocks, pair):
    step = pl.program_id(0)

    @pl.when(step == 0)
    def _():
        out_ref[...] = jnp.zeros_like(out_ref)

    bags, values = [], []
    for block in range(blocks):
        ids = ids_ref[block]
        shift = lax.shift_right_logical(ids, 7) * BITS
        bags.append((ids & (GROUP - 1), lax.shift_left(jnp.ones_like(ids), shift)))
        values.append(x_ref[block, 0:GROUP, :])
    out_ref[...] += block_sum(bags, values, pair)

    @pl.when(step == pl.num_programs(0) - 1)
    def _():
        for field in range(1, FIELDS - 1):
            out_ref[field * GROUP : (field + 1) * GROUP, :] *= 2.0 ** (-BITS * field)


def hot_sum(rows, ids, blocks=16, pair=4):
    count, height, width = rows.shape
    return pl.pallas_call(
        functools.partial(hot_kernel, blocks=blocks, pair=pair),
        grid=(count // blocks,),
        in_specs=[
            pl.BlockSpec((blocks, height, width), lambda i: (i, 0, 0)),
            pl.BlockSpec((blocks, ids.shape[1], GROUP), lambda i: (i, 0, 0)),
        ],
        out_specs=pl.BlockSpec((V, width), lambda i: (0, 0)),
        out_shape=jax.ShapeDtypeStruct((V, width), jnp.float32),
        compiler_params=pltpu.CompilerParams(vmem_limit_bytes=40 << 20),
        cost_estimate=pl.CostEstimate(flops=2 * V * count * GROUP * width, bytes_accessed=3 << 20, transcendentals=0),
        name="hot_sum",
    )(rows, ids)


def cold_kernel(x_ref, hot_ref, out_ref, *, blocks, pair):
    step = pl.program_id(0)

    @pl.when(step == 0)
    def _():
        out_ref[...] = jnp.zeros_like(out_ref)

    bags, values = [], []
    for block in range(blocks):
        code = x_ref[block, GROUP : GROUP + 8, :].astype(jnp.float32)
        bags.append(decode_ids(code))
        values.append(x_ref[block, 0:GROUP, :])
    total = block_sum(bags, values, pair)
    for field in range(FIELDS):
        out_ref[field, 0:GROUP, :] += total[field * GROUP : (field + 1) * GROUP]

    @pl.when(step == pl.num_programs(0) - 1)
    def _():
        for field in range(FIELDS):
            if 0 < field < FIELDS - 1:
                out_ref[field, 0:GROUP, :] *= 2.0 ** (-BITS * field)
            out_ref[field, GROUP:, :] = hot_ref[...]


def cold_sum(rows, hot_rows, blocks=16, pair=4):
    count, height, width = rows.shape
    tall = GROUP + hot_rows.shape[0]
    return pl.pallas_call(
        functools.partial(cold_kernel, blocks=blocks, pair=pair),
        grid=(count // blocks,),
        in_specs=[
            pl.BlockSpec((blocks, height, width), lambda i: (i, 0, 0)),
            pl.BlockSpec(hot_rows.shape, lambda i: (0, 0)),
        ],
        out_specs=pl.BlockSpec((FIELDS, tall, width), lambda i: (0, 0, 0)),
        out_shape=jax.ShapeDtypeStruct((FIELDS, tall, width), jnp.float32),
        compiler_params=pltpu.CompilerParams(vmem_limit_bytes=40 << 20),
        cost_estimate=pl.CostEstimate(flops=2 * V * count * GROUP * width, bytes_accessed=3 << 20, transcendentals=0),
        name="cold_sum",
    )(rows, hot_rows)


def halve(rows, axis, size, bit):
    half = rows.shape[0] // 2
    mine = (lax.axis_index(axis) // bit) % 2
    pairs = [(i, i ^ bit) for i in range(size)]
    got = lax.ppermute(lax.dynamic_slice_in_dim(rows, (1 - mine) * half, half), axis, pairs)
    return lax.dynamic_slice_in_dim(rows, mine * half, half) + got


def double(rows, axis, size, bit):
    mine = (lax.axis_index(axis) // bit) % 2
    got = lax.ppermute(rows, axis, [(i, i ^ bit) for i in range(size)])
    return jnp.where(mine == 0, jnp.concatenate([rows, got], 0), jnp.concatenate([got, rows], 0))


def per_device(pooled_grad, cold_ids, lengths, hot_ids, table, accum, hot_table, hot_accum):
    shards = lax.axis_size("shard")
    bits = [1 << b for b in range(6)]
    rows = jnp.concatenate([jnp.transpose(pooled_grad, (1, 0, 2)), encode_ids(cold_ids, lengths)], 1)
    moved = lax.all_to_all(rows, "shard", split_axis=0, concat_axis=0, tiled=True)
    hot = hot_sum(rows, jnp.transpose(hot_ids, (1, 2, 0)))
    for bit in bits:
        hot = halve(hot, "shard", shards, bit)
    pieces = cold_sum(moved, hot)
    shared = lax.all_to_all(pieces, "rep", split_axis=0, concat_axis=0, tiled=True)
    total = jnp.sum(shared, axis=0)
    cold_total = lax.all_gather(total[:GROUP], "rep", tiled=True)
    hot = total[GROUP:]
    for bit in reversed(bits):
        hot = double(hot, "shard", shards, bit)
    new_table, new_accum = adagrad(table, accum, cold_total)
    new_hot_table, new_hot_accum = adagrad(hot_table, hot_accum, hot)
    return (new_table, new_accum, new_hot_table, new_hot_accum)


def solution(mesh):
    in_specs = (
        P(("shard", "rep"), None, None),
        P(("shard", "rep"), None, None),
        P(("shard", "rep"), None),
        P(("shard", "rep"), None, None),
        P("shard", None),
        P("shard"),
        P(),
        P(),
    )
    out_specs = (P("shard", None), P("shard"), P(), P())
    return jax.shard_map(
        per_device, mesh=mesh, in_specs=in_specs, out_specs=out_specs, check_vma=False
    )
```

```python
import functools

import jax
import jax.numpy as jnp
from jax import lax
from jax.experimental import pallas as pl
from jax.experimental.pallas import tpu as pltpu
from jax.sharding import PartitionSpec as P

V = 1024
GROUP = 128
FIELDS = 8
BITS = 4
TILE = 16

learning_rate = 0.5
epsilon = 1e-06

PARAMS = pltpu.CompilerParams(vmem_limit_bytes=40 << 20)


def encode_ids(cold_ids, lengths):
    ids = jnp.transpose(cold_ids, (1, 2, 0))
    used = jnp.transpose(lengths, (1, 0))[:, None, :]
    position = lax.broadcasted_iota(jnp.int32, ids.shape, 1)
    low, high = ids & (GROUP - 1), ids >> 7
    return jnp.where(position < used, (GROUP + low) << high, 0).astype(jnp.bfloat16)


def decode_ids(code):
    key = jnp.zeros(code.shape, jnp.float32)
    unit = jnp.zeros(code.shape, jnp.int32)
    for field in range(FIELDS):
        reached = code >= float(GROUP * 2**field)
        key = jnp.where(reached, code * 2.0**-field - float(GROUP), key)
        unit = jnp.where(reached, 1 << (BITS * field), unit)
    return key.astype(jnp.int32), unit


def packed_counts(key, unit):
    rows = lax.broadcasted_iota(jnp.int32, (GROUP, key.shape[1]), 0)
    total = jnp.where(rows == key[0:1], unit[0:1], 0)
    for slot in range(1, key.shape[0]):
        total = total + jnp.where(rows == key[slot : slot + 1], unit[slot : slot + 1], 0)
    return total


def unpacked_counts(packed):
    groups = []
    for field in range(FIELDS):
        if field == FIELDS - 1:
            part = lax.shift_right_logical(packed, jnp.int32(BITS * field))
        else:
            part = packed & jnp.int32(((1 << BITS) - 1) << (BITS * field))
        groups.append(part.astype(jnp.float32).astype(jnp.bfloat16))
    return jnp.concatenate(groups, 0)


def field_scale(field):
    return 2.0 ** (-BITS * field) if field < FIELDS - 1 else 1.0


def block_sum(bags, values, pair):
    total = None
    for first in range(0, len(bags), pair):
        counts = jnp.concatenate([unpacked_counts(packed_counts(*bag)) for bag in bags[first : first + pair]], 1)
        rows = jnp.concatenate(values[first : first + pair], 0)
        product = jnp.dot(counts, rows, preferred_element_type=jnp.float32)
        total = product if total is None else total + product
    return total


def diagonal(rows):
    shape = (rows, GROUP)
    return lax.broadcasted_iota(jnp.int32, shape, 0) == lax.broadcasted_iota(jnp.int32, shape, 1)


def to_row(column):
    return jnp.sum(jnp.where(diagonal(column.shape[0]), column, 0.0), axis=0, keepdims=True)


def to_column(row, rows=GROUP):
    return jnp.sum(jnp.where(diagonal(rows), row, 0.0), axis=1, keepdims=True)


def quantized(x):
    top = jnp.maximum(jnp.max(jnp.abs(x), axis=1, keepdims=True), 1e-30)
    level = jnp.ceil(8.0 * jnp.log2(top) + 0.05)
    return jnp.round(x * jnp.exp2(15.0 - level * 0.125)).astype(jnp.int32).astype(jnp.int16), level


def restored(codes, level):
    return codes.astype(jnp.int32).astype(jnp.float32) * jnp.exp2(level * 0.125 - 15.0)


def level_tile(level):
    return jnp.broadcast_to(to_row(level), (TILE, GROUP)).astype(jnp.int32).astype(jnp.int16)


def tile_level(tile):
    return to_column(tile.astype(jnp.int32).astype(jnp.float32)[0:1])


def hot_kernel(x_ref, ids_ref, out_ref, *, blocks, pair):
    step = pl.program_id(0)

    @pl.when(step == 0)
    def _():
        out_ref[...] = jnp.zeros_like(out_ref)

    bags, values = [], []
    for block in range(blocks):
        ids = ids_ref[block]
        shift = lax.shift_right_logical(ids, 7) * BITS
        bags.append((ids & (GROUP - 1), lax.shift_left(jnp.ones_like(ids), shift)))
        values.append(x_ref[block, 0:GROUP, :])
    out_ref[...] += block_sum(bags, values, pair)

    @pl.when(step == pl.num_programs(0) - 1)
    def _():
        for field in range(1, FIELDS - 1):
            out_ref[field * GROUP : (field + 1) * GROUP, :] *= field_scale(field)


def hot_sum(rows, ids, blocks=16, pair=4):
    count, height, width = rows.shape
    return pl.pallas_call(
        functools.partial(hot_kernel, blocks=blocks, pair=pair),
        grid=(count // blocks,),
        in_specs=[
            pl.BlockSpec((blocks, height, width), lambda i: (i, 0, 0)),
            pl.BlockSpec((blocks, ids.shape[1], GROUP), lambda i: (i, 0, 0)),
        ],
        out_specs=pl.BlockSpec((V, width), lambda i: (0, 0)),
        out_shape=jax.ShapeDtypeStruct((V, width), jnp.float32),
        compiler_params=PARAMS,
        cost_estimate=pl.CostEstimate(flops=2 * V * count * GROUP * width, bytes_accessed=3 << 20, transcendentals=0),
        name="hot_sum",
    )(rows, ids)


def cold_kernel(x_ref, out_ref, total_ref, *, blocks, pair):
    step = pl.program_id(0)

    @pl.when(step == 0)
    def _():
        total_ref[...] = jnp.zeros_like(total_ref)

    bags, values = [], []
    for block in range(blocks):
        code = x_ref[block, GROUP : GROUP + 8, :].astype(jnp.float32)
        bags.append(decode_ids(code))
        values.append(x_ref[block, 0:GROUP, :])
    total_ref[...] += block_sum(bags, values, pair)

    @pl.when(step == pl.num_programs(0) - 1)
    def _():
        for field in range(FIELDS):
            rows = total_ref[field * GROUP : (field + 1) * GROUP, :] * field_scale(field)
            codes, level = quantized(rows)
            out_ref[field, 0:GROUP, :] = codes
            out_ref[field, GROUP:, :] = level_tile(level)


def cold_sum(rows, blocks=16, pair=4):
    count, height, width = rows.shape
    return pl.pallas_call(
        functools.partial(cold_kernel, blocks=blocks, pair=pair),
        grid=(count // blocks,),
        in_specs=[pl.BlockSpec((blocks, height, width), lambda i: (i, 0, 0))],
        out_specs=pl.BlockSpec((FIELDS, GROUP + TILE, width), lambda i: (0, 0, 0)),
        out_shape=jax.ShapeDtypeStruct((FIELDS, GROUP + TILE, width), jnp.int16),
        scratch_shapes=[pltpu.VMEM((V, width), jnp.float32)],
        compiler_params=PARAMS,
        cost_estimate=pl.CostEstimate(flops=10 * V * count * GROUP * width, bytes_accessed=3 << 20, transcendentals=0),
        name="cold_sum",
    )(rows)


def whole(body, out_shape, name, *operands):
    return pl.pallas_call(body, out_shape=out_shape, compiler_params=PARAMS, name=name)(*operands)


def stored_everywhere(rows, out_ref):
    codes, level = quantized(rows)
    tile = level_tile(level)
    for peer in range(FIELDS):
        out_ref[peer, 0:GROUP, :] = codes
        out_ref[peer, GROUP:, :] = tile


def peer_sum(pieces_ref):
    total = None
    for peer in range(FIELDS):
        piece = restored(pieces_ref[peer, 0:GROUP, :], tile_level(pieces_ref[peer, GROUP:, :]))
        total = piece if total is None else total + piece
    return total


def spread(rows_ref, out_ref):
    stored_everywhere(rows_ref[...], out_ref)


def gathered_total(pieces_ref, out_ref):
    out_ref[...] = peer_sum(pieces_ref)


def replica_total(pieces_ref, out_ref):
    stored_everywhere(peer_sum(pieces_ref), out_ref)


def update_group(group, grad, table_ref, accum_ref, new_table_ref, new_accum_ref):
    rows = slice(group * GROUP, (group + 1) * GROUP)
    fresh = to_column(accum_ref[group : group + 1, :]) + jnp.sum(grad * grad, axis=1, keepdims=True) * (1.0 / GROUP)
    new_table_ref[rows, :] = table_ref[rows, :] - grad * (learning_rate / (jnp.sqrt(fresh) + epsilon))
    new_accum_ref[group : group + 1, :] = to_row(fresh)


def cold_update(codes_ref, table_ref, accum_ref, new_table_ref, new_accum_ref):
    for group in range(FIELDS):
        grad = restored(codes_ref[group, 0:GROUP, :], tile_level(codes_ref[group, GROUP:, :]))
        update_group(group, grad, table_ref, accum_ref, new_table_ref, new_accum_ref)


def hot_update(grad_ref, table_ref, accum_ref, new_table_ref, new_accum_ref):
    for group in range(FIELDS):
        grad = grad_ref[group * GROUP : (group + 1) * GROUP, :]
        update_group(group, grad, table_ref, accum_ref, new_table_ref, new_accum_ref)


def updated(body, name, grad, table, accum):
    shapes = (
        jax.ShapeDtypeStruct(table.shape, jnp.float32),
        jax.ShapeDtypeStruct((FIELDS, GROUP), jnp.float32),
    )
    new_table, new_accum = whole(body, shapes, name, grad, table, accum.reshape(FIELDS, GROUP))
    return new_table, new_accum.reshape(V)


def halve(rows, axis, bit):
    half = rows.shape[0] // 2
    mine = (lax.axis_index(axis) // bit) % 2
    pairs = [(i, i ^ bit) for i in range(lax.axis_size(axis))]
    got = lax.ppermute(lax.dynamic_slice_in_dim(rows, (1 - mine) * half, half), axis, pairs)
    return lax.dynamic_slice_in_dim(rows, mine * half, half) + got


def double(rows, axis, bit):
    mine = (lax.axis_index(axis) // bit) % 2
    got = lax.ppermute(rows, axis, [(i, i ^ bit) for i in range(lax.axis_size(axis))])
    return jnp.where(mine == 0, jnp.concatenate([rows, got], 0), jnp.concatenate([got, rows], 0))


def per_device(pooled_grad, cold_ids, lengths, hot_ids, table, accum, hot_table, hot_accum):
    lines = [[y * 8 + inner for y in range(8)] for inner in range(8)]
    coded = jax.ShapeDtypeStruct((FIELDS, GROUP + TILE, GROUP), jnp.int16)
    rows = jnp.concatenate([jnp.transpose(pooled_grad, (1, 0, 2)), encode_ids(cold_ids, lengths)], 1)
    moved = lax.all_to_all(rows, "shard", split_axis=0, concat_axis=0, tiled=True)
    hot = hot_sum(rows, jnp.transpose(hot_ids, (1, 2, 0)))
    for bit in (1, 2, 4):
        hot = halve(hot, "shard", bit)
    for bit in (1, 2, 4):
        hot = hot + lax.ppermute(hot, "rep", [(i, i ^ bit) for i in range(FIELDS)])
    hot = whole(spread, coded, "spread", hot)
    moved, hot = lax.optimization_barrier((moved, hot))
    hot = lax.all_to_all(hot, "shard", split_axis=0, concat_axis=0, axis_index_groups=lines, tiled=True)
    pieces = cold_sum(moved)
    pieces, hot = lax.optimization_barrier((pieces, hot))
    shared = lax.all_to_all(pieces, "rep", split_axis=0, concat_axis=0, tiled=True)
    hot = whole(gathered_total, jax.ShapeDtypeStruct((GROUP, GROUP), jnp.float32), "gathered_total", hot)
    payload = whole(replica_total, coded, "replica_total", shared)
    codes = lax.all_to_all(payload, "rep", split_axis=0, concat_axis=0, tiled=True)
    for bit in (4, 2, 1):
        hot = double(hot, "shard", bit)
    new_hot_table, new_hot_accum = updated(hot_update, "hot_update", hot, hot_table, hot_accum)
    new_table, new_accum = updated(cold_update, "cold_update", codes, table, accum)
    return (new_table, new_accum, new_hot_table, new_hot_accum)


def solution(mesh):
    in_specs = (
        P(("shard", "rep"), None, None),
        P(("shard", "rep"), None, None),
        P(("shard", "rep"), None),
        P(("shard", "rep"), None, None),
        P("shard", None),
        P("shard"),
        P(),
        P(),
    )
    out_specs = (P("shard", None), P("shard"), P(), P())
    return jax.shard_map(
        per_device, mesh=mesh, in_specs=in_specs, out_specs=out_specs, check_vma=False
    )
```

```python
import functools

import jax
import jax.numpy as jnp
from jax import lax
from jax.experimental import pallas as pl
from jax.experimental.pallas import tpu as pltpu
from jax.sharding import PartitionSpec as P

V = 1024
GROUP = 128
HALF = 64
FIELDS = 8
BITS = 4
TILE = 16
PAIRS = 0x33333333

learning_rate = 0.5
epsilon = 1e-06

PARAMS = pltpu.CompilerParams(vmem_limit_bytes=40 << 20)


def decode_ids(code):
    key = jnp.zeros(code.shape, jnp.float32)
    unit = jnp.zeros(code.shape, jnp.int32)
    for field in range(FIELDS):
        reached = code >= float(GROUP * 2**field)
        key = jnp.where(reached, code * 2.0**-field - float(GROUP), key)
        unit = jnp.where(reached, 1 << (BITS * field), unit)
    upper = key >= float(HALF)
    key = jnp.where(upper, key - float(HALF), key)
    return key.astype(jnp.int32), jnp.where(upper, unit * 4, unit)


def packed_counts(key, unit):
    rows = lax.broadcasted_iota(jnp.int32, (HALF, key.shape[1]), 0)
    even = odd = None
    for first in range(0, key.shape[0], 3):
        total = None
        for slot in range(first, min(first + 3, key.shape[0])):
            term = jnp.where(rows == key[slot : slot + 1], unit[slot : slot + 1], 0)
            total = term if total is None else total + term
        low, high = total & PAIRS, lax.shift_right_logical(total, 2) & PAIRS
        even = low if even is None else even + low
        odd = high if odd is None else odd + high
    return even, odd


def unpacked_counts(even, odd):
    groups = []
    for field in range(FIELDS):
        for packed in (even, odd):
            if field == FIELDS - 1:
                part = lax.shift_right_logical(packed, BITS * field)
            else:
                part = packed & (((1 << BITS) - 1) << (BITS * field))
            groups.append(part.astype(jnp.float32).astype(jnp.bfloat16))
    return jnp.concatenate(groups, 0)


def field_scale(field):
    return 2.0 ** (-BITS * field) if field < FIELDS - 1 else 1.0


def block_sum(bags, values):
    total = None
    for bag, rows in zip(bags, values):
        product = jnp.dot(unpacked_counts(*packed_counts(*bag)), rows, preferred_element_type=jnp.float32)
        total = product if total is None else total + product
    return total


def diagonal(rows):
    shape = (rows, GROUP)
    return lax.broadcasted_iota(jnp.int32, shape, 0) == lax.broadcasted_iota(jnp.int32, shape, 1)


def to_row(column):
    return jnp.sum(jnp.where(diagonal(column.shape[0]), column, 0.0), axis=0, keepdims=True)


def to_column(row, rows=GROUP):
    return jnp.sum(jnp.where(diagonal(rows), row, 0.0), axis=1, keepdims=True)


def quantized(x):
    top = jnp.maximum(jnp.max(jnp.abs(x), axis=1, keepdims=True), 1e-30)
    level = jnp.ceil(8.0 * jnp.log2(top) + 0.05)
    return jnp.round(x * jnp.exp2(15.0 - level * 0.125)).astype(jnp.int32).astype(jnp.int16), level


def restored(codes, level):
    return codes.astype(jnp.int32).astype(jnp.float32) * jnp.exp2(level * 0.125 - 15.0)


def level_tile(level):
    return jnp.broadcast_to(to_row(level), (TILE, GROUP)).astype(jnp.int32).astype(jnp.int16)


def tile_level(tile):
    return to_column(tile.astype(jnp.int32).astype(jnp.float32)[0:1])


def prepare_kernel(grad_ref, ids_ref, lengths_ref, out_ref, grads, ids_buf, lengths_buf, outs, in_sems, out_sems):
    parts, block = grads.shape[0], grads.shape[2]
    samples = grads.shape[1]
    small = (
        pltpu.make_async_copy(lengths_ref, lengths_buf, in_sems.at[parts]),
        pltpu.make_async_copy(ids_ref, ids_buf, in_sems.at[parts + 1]),
    )
    large = [
        pltpu.make_async_copy(grad_ref.at[:, pl.ds(part * block, block), :], grads.at[part], in_sems.at[part])
        for part in range(parts)
    ]
    for copy in small:
        copy.start()
    for copy in large:
        copy.start()
    for copy in small:
        copy.wait()
    ids = ids_buf[...]
    position = lax.broadcasted_iota(jnp.int32, ids.shape, 1)
    code = jnp.where(position < lengths_buf[...][:, None, :], (GROUP + (ids & (GROUP - 1))) << (ids >> 7), 0)
    outs[:, samples:, :] = code.astype(jnp.float32).astype(jnp.bfloat16)
    back = []
    for part in range(parts):
        rows = pl.ds(part * block, block)
        large[part].wait()
        outs[rows, 0:samples, :] = jnp.swapaxes(grads[part], 0, 1)
        back.append(pltpu.make_async_copy(outs.at[rows], out_ref.at[rows], out_sems.at[part]))
        back[part].start()
    for copy in back:
        copy.wait()


def prepare(grad, ids, lengths, parts=4):
    samples, features, width = grad.shape
    slots = ids.shape[1]
    shape = (features, samples + slots, width)
    return pl.pallas_call(
        prepare_kernel,
        in_specs=[pl.BlockSpec(memory_space=pl.ANY)] * 3,
        out_specs=pl.BlockSpec(memory_space=pl.ANY),
        out_shape=jax.ShapeDtypeStruct(shape, jnp.bfloat16),
        scratch_shapes=[
            pltpu.VMEM((parts, samples, features // parts, width), jnp.bfloat16),
            pltpu.VMEM(ids.shape, jnp.int32),
            pltpu.VMEM(lengths.shape, jnp.int32),
            pltpu.VMEM(shape, jnp.bfloat16),
            pltpu.SemaphoreType.DMA((parts + 2,)),
            pltpu.SemaphoreType.DMA((parts,)),
        ],
        compiler_params=pltpu.CompilerParams(vmem_limit_bytes=60 << 20),
        cost_estimate=pl.CostEstimate(flops=0, bytes_accessed=5 << 20, transcendentals=0),
        name="prepare",
    )(grad, ids, lengths)


def hot_kernel(x_ref, ids_ref, out_ref, *, blocks):
    step = pl.program_id(0)

    @pl.when(step == 0)
    def _():
        out_ref[...] = jnp.zeros_like(out_ref)

    bags, values = [], []
    for block in range(blocks):
        ids = ids_ref[block]
        shift = lax.shift_right_logical(ids, 6) * 2
        bags.append((ids & (HALF - 1), lax.shift_left(jnp.ones_like(ids), shift)))
        values.append(x_ref[block, 0:GROUP, :])
    out_ref[...] += block_sum(bags, values)

    @pl.when(step == pl.num_programs(0) - 1)
    def _():
        for field in range(1, FIELDS - 1):
            out_ref[field * GROUP : (field + 1) * GROUP, :] *= field_scale(field)


def hot_sum(rows, ids, blocks=16):
    count, height, width = rows.shape
    return pl.pallas_call(
        functools.partial(hot_kernel, blocks=blocks),
        grid=(count // blocks,),
        in_specs=[
            pl.BlockSpec((blocks, height, width), lambda i: (i, 0, 0)),
            pl.BlockSpec((blocks, ids.shape[1], GROUP), lambda i: (i, 0, 0)),
        ],
        out_specs=pl.BlockSpec((V, width), lambda i: (0, 0)),
        out_shape=jax.ShapeDtypeStruct((V, width), jnp.float32),
        compiler_params=PARAMS,
        cost_estimate=pl.CostEstimate(flops=2 * V * count * GROUP * width, bytes_accessed=3 << 20, transcendentals=0),
        name="hot_sum",
    )(rows, ids)


def cold_kernel(x_ref, out_ref, rows_ref, total_ref, sems, *, blocks):
    parts = x_ref.shape[0] // blocks

    def copy(part):
        at = pl.ds(part * blocks, blocks)
        return pltpu.make_async_copy(x_ref.at[at], rows_ref.at[at], sems.at[part])

    for part in range(parts):
        copy(part).start()
    total_ref[...] = jnp.zeros_like(total_ref)

    def add(part, carry):
        copy(part).wait()
        bags, values = [], []
        for block in range(blocks):
            at = part * blocks + block
            bags.append(decode_ids(rows_ref[at, GROUP : GROUP + 8, :].astype(jnp.float32)))
            values.append(rows_ref[at, 0:GROUP, :])
        total_ref[...] += block_sum(bags, values)
        return carry

    lax.fori_loop(0, parts, add, 0)
    for field in range(FIELDS):
        rows = total_ref[field * GROUP : (field + 1) * GROUP, :] * field_scale(field)
        codes, level = quantized(rows)
        out_ref[field, 0:GROUP, :] = codes
        out_ref[field, GROUP:, :] = level_tile(level)


def cold_sum(rows, blocks=16):
    count, height, width = rows.shape
    return pl.pallas_call(
        functools.partial(cold_kernel, blocks=blocks),
        in_specs=[pl.BlockSpec(memory_space=pl.ANY)],
        out_specs=pl.BlockSpec(memory_space=pltpu.VMEM),
        out_shape=jax.ShapeDtypeStruct((FIELDS, GROUP + TILE, width), jnp.int16),
        scratch_shapes=[
            pltpu.VMEM(rows.shape, rows.dtype),
            pltpu.VMEM((V, width), jnp.float32),
            pltpu.SemaphoreType.DMA((count // blocks,)),
        ],
        compiler_params=PARAMS,
        cost_estimate=pl.CostEstimate(flops=10 * V * count * GROUP * width, bytes_accessed=3 << 20, transcendentals=0),
        name="cold_sum",
    )(rows)


def whole(body, out_shape, name, *operands):
    return pl.pallas_call(body, out_shape=out_shape, compiler_params=PARAMS, name=name)(*operands)


def stored_everywhere(rows, out_ref):
    codes, level = quantized(rows)
    tile = level_tile(level)
    for peer in range(FIELDS):
        out_ref[peer, 0:GROUP, :] = codes
        out_ref[peer, GROUP:, :] = tile


def peer_sum(pieces_ref):
    total = None
    for peer in range(FIELDS):
        piece = restored(pieces_ref[peer, 0:GROUP, :], tile_level(pieces_ref[peer, GROUP:, :]))
        total = piece if total is None else total + piece
    return total


def spread(rows_ref, out_ref):
    stored_everywhere(rows_ref[...], out_ref)


def line_total(pieces_ref, out_ref):
    codes, level = quantized(peer_sum(pieces_ref))
    out_ref[0:GROUP, :] = codes
    out_ref[GROUP:, :] = level_tile(level)


def replica_total(pieces_ref, out_ref):
    stored_everywhere(peer_sum(pieces_ref), out_ref)


def update_group(group, grad, table_ref, accum_ref, new_table_ref, new_accum_ref):
    rows = slice(group * GROUP, (group + 1) * GROUP)
    fresh = to_column(accum_ref[group : group + 1, :]) + jnp.sum(grad * grad, axis=1, keepdims=True) * (1.0 / GROUP)
    new_table_ref[rows, :] = table_ref[rows, :] - grad * (learning_rate / (jnp.sqrt(fresh) + epsilon))
    new_accum_ref[group : group + 1, :] = to_row(fresh)


def update(codes_ref, table_ref, accum_ref, new_table_ref, new_accum_ref):
    for group in range(FIELDS):
        grad = restored(codes_ref[group, 0:GROUP, :], tile_level(codes_ref[group, GROUP:, :]))
        update_group(group, grad, table_ref, accum_ref, new_table_ref, new_accum_ref)


def updated(name, codes, table, accum):
    shapes = (
        jax.ShapeDtypeStruct(table.shape, jnp.float32),
        jax.ShapeDtypeStruct((FIELDS, GROUP), jnp.float32),
    )
    new_table, new_accum = whole(update, shapes, name, codes, table, accum.reshape(FIELDS, GROUP))
    return new_table, new_accum.reshape(V)


def halve(rows, axis, mask, mine):
    half = rows.shape[0] // 2
    pairs = [(i, i ^ mask) for i in range(lax.axis_size(axis))]
    got = lax.ppermute(lax.dynamic_slice_in_dim(rows, (1 - mine) * half, half), axis, pairs)
    return lax.dynamic_slice_in_dim(rows, mine * half, half) + got


def double(rows, axis, mask, mine):
    got = lax.ppermute(rows, axis, [(i, i ^ mask) for i in range(lax.axis_size(axis))])
    return jnp.where(mine == 0, jnp.concatenate([rows, got], 0), jnp.concatenate([got, rows], 0))


def per_device(pooled_grad, cold_ids, lengths, hot_ids, table, accum, hot_table, hot_accum):
    lines = [[y * 8 + inner for y in range(8)] for inner in range(8)]
    coded = jax.ShapeDtypeStruct((FIELDS, GROUP + TILE, GROUP), jnp.int16)
    rows = prepare(pooled_grad, jnp.transpose(cold_ids, (1, 2, 0)), jnp.transpose(lengths, (1, 0)))
    moved = lax.all_to_all(rows, "shard", split_axis=0, concat_axis=0, tiled=True)
    hot = hot_sum(rows, jnp.transpose(hot_ids, (1, 2, 0)))
    me = lax.axis_index("shard")
    core, low, high = me & 1, (me >> 1) & 1, (me >> 2) & 1
    rounds = ((1, core), (6, high), (2, low ^ high))
    for mask, mine in rounds:
        hot = halve(hot, "shard", mask, mine)
    for bit in (1, 2, 4):
        hot = hot + lax.ppermute(hot, "rep", [(i, i ^ bit) for i in range(FIELDS)])
    hot = whole(spread, coded, "spread", hot)
    moved, hot = lax.optimization_barrier((moved, hot))
    hot = lax.all_to_all(hot, "shard", split_axis=0, concat_axis=0, axis_index_groups=lines, tiled=True)
    pieces = cold_sum(moved)
    pieces, hot = lax.optimization_barrier((pieces, hot))
    shared = lax.all_to_all(pieces, "rep", split_axis=0, concat_axis=0, tiled=True)
    hot = whole(line_total, jax.ShapeDtypeStruct(coded.shape[1:], jnp.int16), "line_total", hot)
    payload = whole(replica_total, coded, "replica_total", shared)
    hot = double(hot, "shard", *rounds[2])
    payload, hot = lax.optimization_barrier((payload, hot))
    codes = lax.all_to_all(payload, "rep", split_axis=0, concat_axis=0, tiled=True)
    for mask, mine in rounds[1::-1]:
        hot = double(hot, "shard", mask, mine)
    new_hot_table, new_hot_accum = updated("hot_update", hot.reshape(coded.shape), hot_table, hot_accum)
    new_table, new_accum = updated("cold_update", codes, table, accum)
    return (new_table, new_accum, new_hot_table, new_hot_accum)


def solution(mesh):
    in_specs = (
        P(("shard", "rep"), None, None),
        P(("shard", "rep"), None, None),
        P(("shard", "rep"), None),
        P(("shard", "rep"), None, None),
        P("shard", None),
        P("shard"),
        P(),
        P(),
    )
    out_specs = (P("shard", None), P("shard"), P(), P())
    return jax.shard_map(
        per_device, mesh=mesh, in_specs=in_specs, out_specs=out_specs, check_vma=False
    )
```

```python
import functools

import jax
import jax.numpy as jnp
from jax import lax
from jax.experimental import pallas as pl
from jax.experimental.pallas import tpu as pltpu
from jax.sharding import PartitionSpec as P

V = 1024
GROUP = 128
HALF = 64
FIELDS = 8
BITS = 4
TILE = 8
PAIRS = 0x33333333

learning_rate = 0.5
epsilon = 1e-06

PARAMS = pltpu.CompilerParams(vmem_limit_bytes=40 << 20)


def decode_ids(code):
    key = jnp.zeros(code.shape, jnp.float32)
    unit = jnp.zeros(code.shape, jnp.int32)
    for field in range(FIELDS):
        reached = code >= float(GROUP * 2**field)
        key = jnp.where(reached, code * 2.0**-field - float(GROUP), key)
        unit = jnp.where(reached, 1 << (BITS * field), unit)
    upper = key >= float(HALF)
    key = jnp.where(upper, key - float(HALF), key)
    return key.astype(jnp.int32), jnp.where(upper, unit * 4, unit)


def packed_counts(key, unit):
    rows = lax.broadcasted_iota(jnp.int32, (HALF, key.shape[1]), 0)
    even = odd = None
    for first in range(0, key.shape[0], 3):
        total = None
        for slot in range(first, min(first + 3, key.shape[0])):
            term = jnp.where(rows == key[slot : slot + 1], unit[slot : slot + 1], 0)
            total = term if total is None else total + term
        low, high = total & PAIRS, lax.shift_right_logical(total, 2) & PAIRS
        even = low if even is None else even + low
        odd = high if odd is None else odd + high
    return even, odd


def unpacked_counts(even, odd):
    groups = []
    for field in range(FIELDS):
        for packed in (even, odd):
            if field == FIELDS - 1:
                part = lax.shift_right_logical(packed, BITS * field)
            else:
                part = packed & (((1 << BITS) - 1) << (BITS * field))
            groups.append(part.astype(jnp.float32).astype(jnp.bfloat16))
    return jnp.concatenate(groups, 0)


def field_scale(field):
    return 2.0 ** (-BITS * field) if field < FIELDS - 1 else 1.0


def block_sum(bags, values):
    total = None
    for bag, rows in zip(bags, values):
        product = jnp.dot(unpacked_counts(*packed_counts(*bag)), rows, preferred_element_type=jnp.float32)
        total = product if total is None else total + product
    return total


def diagonal(rows):
    shape = (rows, GROUP)
    return lax.broadcasted_iota(jnp.int32, shape, 0) == lax.broadcasted_iota(jnp.int32, shape, 1)


def to_row(column):
    return jnp.sum(jnp.where(diagonal(column.shape[0]), column, 0.0), axis=0, keepdims=True)


def to_column(row, rows=GROUP):
    return jnp.sum(jnp.where(diagonal(rows), row, 0.0), axis=1, keepdims=True)


def quantized(x):
    top = jnp.maximum(jnp.max(jnp.abs(x), axis=1, keepdims=True), 1e-30)
    level = jnp.ceil(8.0 * jnp.log2(top) + 0.05)
    return jnp.round(x * jnp.exp2(15.0 - level * 0.125)).astype(jnp.int32).astype(jnp.int16), level


def restored(codes, level):
    return codes.astype(jnp.int32).astype(jnp.float32) * jnp.exp2(level * 0.125 - 15.0)


def level_tile(level):
    return jnp.broadcast_to(to_row(level), (TILE, GROUP)).astype(jnp.int32).astype(jnp.int16)


def tile_level(tile):
    return to_column(tile.astype(jnp.int32).astype(jnp.float32)[0:1])


def prepare_kernel(grad_ref, ids_ref, lengths_ref, out_ref, grads, ids_buf, lengths_buf, outs, in_sems, out_sems):
    parts, block = grads.shape[0], grads.shape[2]
    samples = grads.shape[1]
    small = (
        pltpu.make_async_copy(lengths_ref, lengths_buf, in_sems.at[parts]),
        pltpu.make_async_copy(ids_ref, ids_buf, in_sems.at[parts + 1]),
    )
    large = [
        pltpu.make_async_copy(grad_ref.at[:, pl.ds(part * block, block), :], grads.at[part], in_sems.at[part])
        for part in range(parts)
    ]
    for copy in small:
        copy.start()
    for copy in large:
        copy.start()
    for copy in small:
        copy.wait()
    ids = ids_buf[...]
    position = lax.broadcasted_iota(jnp.int32, ids.shape, 1)
    code = jnp.where(position < lengths_buf[...][:, None, :], (GROUP + (ids & (GROUP - 1))) << (ids >> 7), 0)
    outs[:, samples:, :] = code.astype(jnp.float32).astype(jnp.bfloat16)
    back = []
    for part in range(parts):
        rows = pl.ds(part * block, block)
        large[part].wait()
        outs[rows, 0:samples, :] = jnp.swapaxes(grads[part], 0, 1)
        back.append(pltpu.make_async_copy(outs.at[rows], out_ref.at[rows], out_sems.at[part]))
        back[part].start()
    for copy in back:
        copy.wait()


def prepare(grad, ids, lengths, parts=4):
    samples, features, width = grad.shape
    slots = ids.shape[1]
    shape = (features, samples + slots, width)
    return pl.pallas_call(
        prepare_kernel,
        in_specs=[pl.BlockSpec(memory_space=pl.ANY)] * 3,
        out_specs=pl.BlockSpec(memory_space=pl.ANY),
        out_shape=jax.ShapeDtypeStruct(shape, jnp.bfloat16),
        scratch_shapes=[
            pltpu.VMEM((parts, samples, features // parts, width), jnp.bfloat16),
            pltpu.VMEM(ids.shape, jnp.int32),
            pltpu.VMEM(lengths.shape, jnp.int32),
            pltpu.VMEM(shape, jnp.bfloat16),
            pltpu.SemaphoreType.DMA((parts + 2,)),
            pltpu.SemaphoreType.DMA((parts,)),
        ],
        compiler_params=pltpu.CompilerParams(vmem_limit_bytes=60 << 20),
        cost_estimate=pl.CostEstimate(flops=0, bytes_accessed=5 << 20, transcendentals=0),
        name="prepare",
    )(grad, ids, lengths)


def hot_kernel(x_ref, ids_ref, out_ref, *, blocks):
    step = pl.program_id(0)

    @pl.when(step == 0)
    def _():
        out_ref[...] = jnp.zeros_like(out_ref)

    bags, values = [], []
    for block in range(blocks):
        ids = ids_ref[block]
        shift = lax.shift_right_logical(ids, 6) * 2
        bags.append((ids & (HALF - 1), lax.shift_left(jnp.ones_like(ids), shift)))
        values.append(x_ref[block, 0:GROUP, :])
    out_ref[...] += block_sum(bags, values)

    @pl.when(step == pl.num_programs(0) - 1)
    def _():
        for field in range(1, FIELDS - 1):
            out_ref[field * GROUP : (field + 1) * GROUP, :] *= field_scale(field)


def hot_sum(rows, ids, blocks=16):
    count, height, width = rows.shape
    return pl.pallas_call(
        functools.partial(hot_kernel, blocks=blocks),
        grid=(count // blocks,),
        in_specs=[
            pl.BlockSpec((blocks, height, width), lambda i: (i, 0, 0)),
            pl.BlockSpec((blocks, ids.shape[1], GROUP), lambda i: (i, 0, 0)),
        ],
        out_specs=pl.BlockSpec((V, width), lambda i: (0, 0)),
        out_shape=jax.ShapeDtypeStruct((V, width), jnp.float32),
        compiler_params=PARAMS,
        cost_estimate=pl.CostEstimate(flops=2 * V * count * GROUP * width, bytes_accessed=3 << 20, transcendentals=0),
        name="hot_sum",
    )(rows, ids)


def cold_kernel(x_ref, out_ref, rows_ref, total_ref, sems, *, blocks):
    parts = x_ref.shape[0] // blocks

    def copy(part):
        at = pl.ds(part * blocks, blocks)
        return pltpu.make_async_copy(x_ref.at[at], rows_ref.at[at], sems.at[part])

    for part in range(parts):
        copy(part).start()
    total_ref[...] = jnp.zeros_like(total_ref)

    def add(part, carry):
        copy(part).wait()
        bags, values = [], []
        for block in range(blocks):
            at = part * blocks + block
            bags.append(decode_ids(rows_ref[at, GROUP : GROUP + 8, :].astype(jnp.float32)))
            values.append(rows_ref[at, 0:GROUP, :])
        total_ref[...] += block_sum(bags, values)
        return carry

    lax.fori_loop(0, parts, add, 0)
    for field in range(FIELDS):
        rows = total_ref[field * GROUP : (field + 1) * GROUP, :] * field_scale(field)
        codes, level = quantized(rows)
        out_ref[field, 0:GROUP, :] = codes
        out_ref[field, GROUP:, :] = level_tile(level)


def cold_sum(rows, blocks=16):
    count, height, width = rows.shape
    return pl.pallas_call(
        functools.partial(cold_kernel, blocks=blocks),
        in_specs=[pl.BlockSpec(memory_space=pl.ANY)],
        out_specs=pl.BlockSpec(memory_space=pltpu.VMEM),
        out_shape=jax.ShapeDtypeStruct((FIELDS, GROUP + TILE, width), jnp.int16),
        scratch_shapes=[
            pltpu.VMEM(rows.shape, rows.dtype),
            pltpu.VMEM((V, width), jnp.float32),
            pltpu.SemaphoreType.DMA((count // blocks,)),
        ],
        compiler_params=PARAMS,
        cost_estimate=pl.CostEstimate(flops=10 * V * count * GROUP * width, bytes_accessed=3 << 20, transcendentals=0),
        name="cold_sum",
    )(rows)


def whole(body, out_shape, name, *operands):
    return pl.pallas_call(body, out_shape=out_shape, compiler_params=PARAMS, name=name)(*operands)


def stored_everywhere(rows, out_ref):
    codes, level = quantized(rows)
    tile = level_tile(level)
    for peer in range(FIELDS):
        out_ref[peer, 0:GROUP, :] = codes
        out_ref[peer, GROUP:, :] = tile


def peer_sum(pieces_ref):
    total = None
    for peer in range(FIELDS):
        piece = restored(pieces_ref[peer, 0:GROUP, :], tile_level(pieces_ref[peer, GROUP:, :]))
        total = piece if total is None else total + piece
    return total


def spread(rows_ref, out_ref):
    stored_everywhere(rows_ref[...], out_ref)


def line_total(pieces_ref, out_ref):
    codes, level = quantized(peer_sum(pieces_ref))
    out_ref[0:GROUP, :] = codes
    out_ref[GROUP:, :] = level_tile(level)


def replica_total(pieces_ref, out_ref):
    stored_everywhere(peer_sum(pieces_ref), out_ref)


def update_group(group, grad, table_ref, accum_ref, new_table_ref, new_accum_ref):
    rows = slice(group * GROUP, (group + 1) * GROUP)
    fresh = to_column(accum_ref[group : group + 1, :]) + jnp.sum(grad * grad, axis=1, keepdims=True) * (1.0 / GROUP)
    new_table_ref[rows, :] = table_ref[rows, :] - grad * (learning_rate / (jnp.sqrt(fresh) + epsilon))
    new_accum_ref[group : group + 1, :] = to_row(fresh)


def update(codes_ref, table_ref, accum_ref, new_table_ref, new_accum_ref):
    for group in range(FIELDS):
        grad = restored(codes_ref[group, 0:GROUP, :], tile_level(codes_ref[group, GROUP:, :]))
        update_group(group, grad, table_ref, accum_ref, new_table_ref, new_accum_ref)


def updated(name, codes, table, accum):
    shapes = (
        jax.ShapeDtypeStruct(table.shape, jnp.float32),
        jax.ShapeDtypeStruct((FIELDS, GROUP), jnp.float32),
    )
    new_table, new_accum = whole(update, shapes, name, codes, table, accum.reshape(FIELDS, GROUP))
    return new_table, new_accum.reshape(V)


def halve(rows, axis, mask, mine):
    half = rows.shape[0] // 2
    pairs = [(i, i ^ mask) for i in range(lax.axis_size(axis))]
    got = lax.ppermute(lax.dynamic_slice_in_dim(rows, (1 - mine) * half, half), axis, pairs)
    return lax.dynamic_slice_in_dim(rows, mine * half, half) + got


def double(rows, axis, mask, mine):
    got = lax.ppermute(rows, axis, [(i, i ^ mask) for i in range(lax.axis_size(axis))])
    return jnp.where(mine == 0, jnp.concatenate([rows, got], 0), jnp.concatenate([got, rows], 0))


def per_device(pooled_grad, cold_ids, lengths, hot_ids, table, accum, hot_table, hot_accum):
    lines = [[y * 8 + inner for y in range(8)] for inner in range(8)]
    coded = jax.ShapeDtypeStruct((FIELDS, GROUP + TILE, GROUP), jnp.int16)
    rows = prepare(pooled_grad, jnp.transpose(cold_ids, (1, 2, 0)), jnp.transpose(lengths, (1, 0)))
    moved = lax.all_to_all(rows, "shard", split_axis=0, concat_axis=0, tiled=True)
    hot = hot_sum(rows, jnp.transpose(hot_ids, (1, 2, 0)))
    me = lax.axis_index("shard")
    core, low, high = me & 1, (me >> 1) & 1, (me >> 2) & 1
    rounds = ((1, core), (6, high), (2, low ^ high))
    for mask, mine in rounds:
        hot = halve(hot, "shard", mask, mine)
    for bit in (1, 2, 4):
        hot = hot + lax.ppermute(hot, "rep", [(i, i ^ bit) for i in range(FIELDS)])
    hot = whole(spread, coded, "spread", hot)
    moved, hot = lax.optimization_barrier((moved, hot))
    hot = lax.all_to_all(hot, "shard", split_axis=0, concat_axis=0, axis_index_groups=lines, tiled=True)
    pieces = cold_sum(moved)
    pieces, hot = lax.optimization_barrier((pieces, hot))
    shared = lax.all_to_all(pieces, "rep", split_axis=0, concat_axis=0, tiled=True)
    hot = whole(line_total, jax.ShapeDtypeStruct(coded.shape[1:], jnp.int16), "line_total", hot)
    payload = whole(replica_total, coded, "replica_total", shared)
    hot = double(hot, "shard", *rounds[2])
    codes = lax.all_to_all(payload, "rep", split_axis=0, concat_axis=0, tiled=True)
    for mask, mine in rounds[1::-1]:
        hot = double(hot, "shard", mask, mine)
    new_hot_table, new_hot_accum = updated("hot_update", hot.reshape(coded.shape), hot_table, hot_accum)
    new_table, new_accum = updated("cold_update", codes, table, accum)
    return (new_table, new_accum, new_hot_table, new_hot_accum)


def solution(mesh):
    in_specs = (
        P(("shard", "rep"), None, None),
        P(("shard", "rep"), None, None),
        P(("shard", "rep"), None),
        P(("shard", "rep"), None, None),
        P("shard", None),
        P("shard"),
        P(),
        P(),
    )
    out_specs = (P("shard", None), P("shard"), P(), P())
    return jax.shard_map(
        per_device, mesh=mesh, in_specs=in_specs, out_specs=out_specs, check_vma=False
    )
```

```python
import functools

import jax
import jax.numpy as jnp
from jax import lax
from jax.experimental import pallas as pl
from jax.experimental.pallas import tpu as pltpu
from jax.sharding import PartitionSpec as P

V = 1024
GROUP = 128
HALF = 64
FIELDS = 8
BITS = 4
TILE = 8
PAIRS = 0x33333333

learning_rate = 0.5
epsilon = 1e-06

PARAMS = pltpu.CompilerParams(vmem_limit_bytes=40 << 20)


def decode_ids(code):
    key = jnp.zeros(code.shape, jnp.float32)
    unit = jnp.zeros(code.shape, jnp.int32)
    for field in range(FIELDS):
        reached = code >= float(GROUP * 2**field)
        key = jnp.where(reached, code * 2.0**-field - float(GROUP), key)
        unit = jnp.where(reached, 1 << (BITS * field), unit)
    upper = key >= float(HALF)
    key = jnp.where(upper, key - float(HALF), key)
    return key.astype(jnp.int32), jnp.where(upper, unit * 4, unit)


def packed_counts(key, unit):
    rows = lax.broadcasted_iota(jnp.int32, (HALF, key.shape[1]), 0)
    even = odd = None
    for first in range(0, key.shape[0], 3):
        total = None
        for slot in range(first, min(first + 3, key.shape[0])):
            term = jnp.where(rows == key[slot : slot + 1], unit[slot : slot + 1], 0)
            total = term if total is None else total + term
        low, high = total & PAIRS, lax.shift_right_logical(total, 2) & PAIRS
        even = low if even is None else even + low
        odd = high if odd is None else odd + high
    return even, odd


def unpacked_counts(even, odd):
    groups = []
    for field in range(FIELDS):
        for packed in (even, odd):
            if field == FIELDS - 1:
                part = lax.shift_right_logical(packed, BITS * field)
            else:
                part = packed & (((1 << BITS) - 1) << (BITS * field))
            groups.append(part.astype(jnp.float32).astype(jnp.bfloat16))
    return jnp.concatenate(groups, 0)


def field_scale(field):
    return 2.0 ** (-BITS * field) if field < FIELDS - 1 else 1.0


def block_sum(bags, values):
    total = None
    for bag, rows in zip(bags, values):
        product = jnp.dot(unpacked_counts(*packed_counts(*bag)), rows, preferred_element_type=jnp.float32)
        total = product if total is None else total + product
    return total


def diagonal(rows):
    shape = (rows, GROUP)
    return lax.broadcasted_iota(jnp.int32, shape, 0) == lax.broadcasted_iota(jnp.int32, shape, 1)


def to_row(column):
    return jnp.sum(jnp.where(diagonal(column.shape[0]), column, 0.0), axis=0, keepdims=True)


def to_column(row, rows=GROUP):
    return jnp.sum(jnp.where(diagonal(rows), row, 0.0), axis=1, keepdims=True)


def quantized(x):
    top = jnp.maximum(jnp.max(jnp.abs(x), axis=1, keepdims=True), 1e-30)
    level = jnp.ceil(8.0 * jnp.log2(top) + 0.05)
    return jnp.round(x * jnp.exp2(15.0 - level * 0.125)).astype(jnp.int32).astype(jnp.int16), level


def as_float(codes):
    return codes.astype(jnp.int32).astype(jnp.float32)


def row_scales(tile):
    return jnp.exp2(as_float(tile)[0:1] * 0.125 - 15.0)


def level_tile(level):
    return jnp.broadcast_to(to_row(level), (TILE, GROUP)).astype(jnp.int32).astype(jnp.int16)


def prepare_kernel(grad_ref, ids_ref, lengths_ref, out_ref, grads, ids_buf, lengths_buf, outs, in_sems, out_sems):
    parts, block = grads.shape[0], grads.shape[2]
    samples = grads.shape[1]
    small = (
        pltpu.make_async_copy(lengths_ref, lengths_buf, in_sems.at[parts]),
        pltpu.make_async_copy(ids_ref, ids_buf, in_sems.at[parts + 1]),
    )
    large = [
        pltpu.make_async_copy(grad_ref.at[:, pl.ds(part * block, block), :], grads.at[part], in_sems.at[part])
        for part in range(parts)
    ]
    for copy in small:
        copy.start()
    for copy in large:
        copy.start()
    for copy in small:
        copy.wait()
    ids = ids_buf[...]
    position = lax.broadcasted_iota(jnp.int32, ids.shape, 1)
    code = jnp.where(position < lengths_buf[...][:, None, :], (GROUP + (ids & (GROUP - 1))) << (ids >> 7), 0)
    outs[:, samples:, :] = code.astype(jnp.float32).astype(jnp.bfloat16)
    back = []
    for part in range(parts):
        rows = pl.ds(part * block, block)
        large[part].wait()
        outs[rows, 0:samples, :] = jnp.swapaxes(grads[part], 0, 1)
        back.append(pltpu.make_async_copy(outs.at[rows], out_ref.at[rows], out_sems.at[part]))
        back[part].start()
    for copy in back:
        copy.wait()


def prepare(grad, ids, lengths, parts=4):
    samples, features, width = grad.shape
    slots = ids.shape[1]
    shape = (features, samples + slots, width)
    return pl.pallas_call(
        prepare_kernel,
        in_specs=[pl.BlockSpec(memory_space=pl.ANY)] * 3,
        out_specs=pl.BlockSpec(memory_space=pl.ANY),
        out_shape=jax.ShapeDtypeStruct(shape, jnp.bfloat16),
        scratch_shapes=[
            pltpu.VMEM((parts, samples, features // parts, width), jnp.bfloat16),
            pltpu.VMEM(ids.shape, jnp.int32),
            pltpu.VMEM(lengths.shape, jnp.int32),
            pltpu.VMEM(shape, jnp.bfloat16),
            pltpu.SemaphoreType.DMA((parts + 2,)),
            pltpu.SemaphoreType.DMA((parts,)),
        ],
        compiler_params=pltpu.CompilerParams(vmem_limit_bytes=60 << 20),
        cost_estimate=pl.CostEstimate(flops=0, bytes_accessed=5 << 20, transcendentals=0),
        name="prepare",
    )(grad, ids, lengths)


def hot_kernel(x_ref, ids_ref, out_ref, *, blocks):
    step = pl.program_id(0)

    @pl.when(step == 0)
    def _():
        out_ref[...] = jnp.zeros_like(out_ref)

    bags, values = [], []
    for block in range(blocks):
        ids = ids_ref[block]
        shift = lax.shift_right_logical(ids, 6) * 2
        bags.append((ids & (HALF - 1), lax.shift_left(jnp.ones_like(ids), shift)))
        values.append(x_ref[block, 0:GROUP, :])
    out_ref[...] += block_sum(bags, values)

    @pl.when(step == pl.num_programs(0) - 1)
    def _():
        for field in range(1, FIELDS - 1):
            out_ref[field * GROUP : (field + 1) * GROUP, :] *= field_scale(field)


def hot_sum(rows, ids, blocks=32):
    count, height, width = rows.shape
    return pl.pallas_call(
        functools.partial(hot_kernel, blocks=blocks),
        grid=(count // blocks,),
        in_specs=[
            pl.BlockSpec((blocks, height, width), lambda i: (i, 0, 0)),
            pl.BlockSpec((blocks, ids.shape[1], GROUP), lambda i: (i, 0, 0)),
        ],
        out_specs=pl.BlockSpec((V, width), lambda i: (0, 0)),
        out_shape=jax.ShapeDtypeStruct((V, width), jnp.float32),
        compiler_params=PARAMS,
        cost_estimate=pl.CostEstimate(flops=2 * V * count * GROUP * width, bytes_accessed=3 << 20, transcendentals=0),
        name="hot_sum",
    )(rows, ids)


def cold_kernel(x_ref, out_ref, rows_ref, total_ref, sems, *, blocks):
    parts = x_ref.shape[0] // blocks

    def copy(part):
        at = pl.ds(part * blocks, blocks)
        return pltpu.make_async_copy(x_ref.at[at], rows_ref.at[at], sems.at[part])

    for part in range(parts):
        copy(part).start()
    total_ref[...] = jnp.zeros_like(total_ref)

    def add(part, carry):
        copy(part).wait()
        bags, values = [], []
        for block in range(blocks):
            at = part * blocks + block
            bags.append(decode_ids(rows_ref[at, GROUP : GROUP + 8, :].astype(jnp.float32)))
            values.append(rows_ref[at, 0:GROUP, :])
        total_ref[...] += block_sum(bags, values)
        return carry

    lax.fori_loop(0, parts, add, 0)
    for field in range(FIELDS):
        rows = total_ref[field * GROUP : (field + 1) * GROUP, :] * field_scale(field)
        codes, level = quantized(rows)
        out_ref[field, 0:GROUP, :] = codes
        out_ref[field, GROUP:, :] = level_tile(level)


def cold_sum(rows, blocks=16):
    count, height, width = rows.shape
    return pl.pallas_call(
        functools.partial(cold_kernel, blocks=blocks),
        in_specs=[pl.BlockSpec(memory_space=pl.ANY)],
        out_specs=pl.BlockSpec(memory_space=pltpu.VMEM),
        out_shape=jax.ShapeDtypeStruct((FIELDS, GROUP + TILE, width), jnp.int16),
        scratch_shapes=[
            pltpu.VMEM(rows.shape, rows.dtype),
            pltpu.VMEM((V, width), jnp.float32),
            pltpu.SemaphoreType.DMA((count // blocks,)),
        ],
        compiler_params=PARAMS,
        cost_estimate=pl.CostEstimate(flops=10 * V * count * GROUP * width, bytes_accessed=3 << 20, transcendentals=0),
        name="cold_sum",
    )(rows)


def whole(body, out_shape, name, *operands):
    return pl.pallas_call(body, out_shape=out_shape, compiler_params=PARAMS, name=name)(*operands)


def stored_everywhere(rows, out_ref):
    codes, level = quantized(rows)
    tile = level_tile(level)
    for peer in range(FIELDS):
        out_ref[peer, 0:GROUP, :] = codes
        out_ref[peer, GROUP:, :] = tile


def peer_sum(pieces_ref):
    total = None
    for peer in range(FIELDS):
        piece = as_float(pieces_ref[peer, 0:GROUP, :]) * to_column(row_scales(pieces_ref[peer, GROUP:, :]))
        total = piece if total is None else total + piece
    return total


def spread(rows_ref, out_ref):
    stored_everywhere(rows_ref[...], out_ref)


def line_total(pieces_ref, out_ref):
    codes, level = quantized(peer_sum(pieces_ref))
    out_ref[0:GROUP, :] = codes
    out_ref[GROUP:, :] = level_tile(level)


def replica_total(pieces_ref, out_ref):
    stored_everywhere(peer_sum(pieces_ref), out_ref)


def update(codes_ref, table_ref, accum_ref, new_table_ref, new_accum_ref):
    for group in range(FIELDS):
        rows, one = slice(group * GROUP, (group + 1) * GROUP), slice(group, group + 1)
        codes = as_float(codes_ref[group, 0:GROUP, :])
        scales = row_scales(codes_ref[group, GROUP:, :])
        squares = to_row(jnp.sum(codes * codes, axis=1, keepdims=True))
        fresh = accum_ref[one, :] + squares * scales * scales * (1.0 / GROUP)
        step = to_column(scales * (learning_rate / (jnp.sqrt(fresh) + epsilon)))
        new_accum_ref[one, :] = fresh
        new_table_ref[rows, :] = table_ref[rows, :] - codes * step


def updated(name, codes, table, accum):
    shapes = (
        jax.ShapeDtypeStruct(table.shape, jnp.float32),
        jax.ShapeDtypeStruct((FIELDS, GROUP), jnp.float32),
    )
    new_table, new_accum = whole(update, shapes, name, codes, table, accum.reshape(FIELDS, GROUP))
    return new_table, new_accum.reshape(V)


def halve(rows, axis, mask, mine):
    half = rows.shape[0] // 2
    pairs = [(i, i ^ mask) for i in range(lax.axis_size(axis))]
    got = lax.ppermute(lax.dynamic_slice_in_dim(rows, (1 - mine) * half, half), axis, pairs)
    return lax.dynamic_slice_in_dim(rows, mine * half, half) + got


def double(rows, axis, mask, mine):
    got = lax.ppermute(rows, axis, [(i, i ^ mask) for i in range(lax.axis_size(axis))])
    return jnp.where(mine == 0, jnp.concatenate([rows, got], 0), jnp.concatenate([got, rows], 0))


def per_device(pooled_grad, cold_ids, lengths, hot_ids, table, accum, hot_table, hot_accum):
    lines = [[y * 8 + inner for y in range(8)] for inner in range(8)]
    coded = jax.ShapeDtypeStruct((FIELDS, GROUP + TILE, GROUP), jnp.int16)
    rows = prepare(pooled_grad, jnp.transpose(cold_ids, (1, 2, 0)), jnp.transpose(lengths, (1, 0)))
    moved = lax.all_to_all(rows, "shard", split_axis=0, concat_axis=0, tiled=True)
    hot = hot_sum(rows, jnp.transpose(hot_ids, (1, 2, 0)))
    me = lax.axis_index("shard")
    core, low, high = me & 1, (me >> 1) & 1, (me >> 2) & 1
    rounds = ((1, core), (6, high), (2, low ^ high))
    for mask, mine in rounds:
        hot = halve(hot, "shard", mask, mine)
    for bit in (1, 2, 4):
        hot = hot + lax.ppermute(hot, "rep", [(i, i ^ bit) for i in range(FIELDS)])
    hot = whole(spread, coded, "spread", hot)
    moved, hot = lax.optimization_barrier((moved, hot))
    hot = lax.all_to_all(hot, "shard", split_axis=0, concat_axis=0, axis_index_groups=lines, tiled=True)
    pieces = cold_sum(moved)
    pieces, hot = lax.optimization_barrier((pieces, hot))
    shared = lax.all_to_all(pieces, "rep", split_axis=0, concat_axis=0, tiled=True)
    hot = whole(line_total, jax.ShapeDtypeStruct(coded.shape[1:], jnp.int16), "line_total", hot)
    payload = whole(replica_total, coded, "replica_total", shared)
    hot = double(hot, "shard", *rounds[2])
    codes = lax.all_to_all(payload, "rep", split_axis=0, concat_axis=0, tiled=True)
    for mask, mine in rounds[1::-1]:
        hot = double(hot, "shard", mask, mine)
    new_hot_table, new_hot_accum = updated("hot_update", hot.reshape(coded.shape), hot_table, hot_accum)
    new_table, new_accum = updated("cold_update", codes, table, accum)
    return (new_table, new_accum, new_hot_table, new_hot_accum)


def solution(mesh):
    in_specs = (
        P(("shard", "rep"), None, None),
        P(("shard", "rep"), None, None),
        P(("shard", "rep"), None),
        P(("shard", "rep"), None, None),
        P("shard", None),
        P("shard"),
        P(),
        P(),
    )
    out_specs = (P("shard", None), P("shard"), P(), P())
    return jax.shard_map(
        per_device, mesh=mesh, in_specs=in_specs, out_specs=out_specs, check_vma=False
    )
```

```python
import functools

import jax
import jax.numpy as jnp
from jax import lax
from jax.experimental import pallas as pl
from jax.experimental.pallas import tpu as pltpu
from jax.sharding import PartitionSpec as P

V = 1024
GROUP = 128
HALF = 64
FIELDS = 8
BITS = 4
TILE = 8
PAIRS = 0x33333333

learning_rate = 0.5
epsilon = 1e-06

PARAMS = pltpu.CompilerParams(vmem_limit_bytes=40 << 20)


def decode_ids(code):
    number = code.astype(jnp.int32)
    zeros = lax.clz(number)
    low = lax.shift_right_logical(number, 24 - zeros)
    bit = 4 * (24 - zeros) + (lax.shift_right_logical(low, 5) & 2)
    return low & (HALF - 1), jnp.where(number > 0, lax.shift_left(jnp.ones_like(number), bit), 0)


def packed_counts(key, unit):
    rows = lax.broadcasted_iota(jnp.int32, (HALF, key.shape[1]), 0)
    even = odd = None
    for first in range(0, key.shape[0], 3):
        total = None
        for slot in range(first, min(first + 3, key.shape[0])):
            term = jnp.where(rows == key[slot : slot + 1], unit[slot : slot + 1], 0)
            total = term if total is None else total + term
        low, high = total & PAIRS, lax.shift_right_logical(total, 2) & PAIRS
        even = low if even is None else even + low
        odd = high if odd is None else odd + high
    return even, odd


def unpacked_counts(even, odd):
    groups = []
    for field in range(FIELDS):
        for packed in (even, odd):
            if field == FIELDS - 1:
                part = lax.shift_right_logical(packed, BITS * field)
            else:
                part = packed & (((1 << BITS) - 1) << (BITS * field))
            groups.append(part.astype(jnp.float32).astype(jnp.bfloat16))
    return jnp.concatenate(groups, 0)


def field_scale(field):
    return 2.0 ** (-BITS * field) if field < FIELDS - 1 else 1.0


def block_sum(bags, values):
    total = None
    for bag, rows in zip(bags, values):
        product = jnp.dot(unpacked_counts(*packed_counts(*bag)), rows, preferred_element_type=jnp.float32)
        total = product if total is None else total + product
    return total


def diagonal(rows):
    shape = (rows, GROUP)
    return lax.broadcasted_iota(jnp.int32, shape, 0) == lax.broadcasted_iota(jnp.int32, shape, 1)


def to_row(column):
    return jnp.sum(jnp.where(diagonal(column.shape[0]), column, 0.0), axis=0, keepdims=True)


def to_column(row, rows=GROUP):
    return jnp.sum(jnp.where(diagonal(rows), row, 0.0), axis=1, keepdims=True)


def quantized(x):
    top = jnp.maximum(jnp.max(jnp.abs(x), axis=1, keepdims=True), 1e-30)
    level = jnp.ceil(8.0 * jnp.log2(top) + 0.05)
    return jnp.round(x * jnp.exp2(15.0 - level * 0.125)).astype(jnp.int32).astype(jnp.int16), level


def quantized_in_row(x):
    top = jnp.maximum(to_row(jnp.max(jnp.abs(x), axis=1, keepdims=True)), 1e-30)
    level = jnp.ceil(8.0 * jnp.log2(top) + 0.05)
    scaled = x * to_column(jnp.exp2(15.0 - level * 0.125))
    return jnp.round(scaled).astype(jnp.int32).astype(jnp.int16), level


def row_tile(level):
    return jnp.broadcast_to(level, (TILE, GROUP)).astype(jnp.int32).astype(jnp.int16)


def as_float(codes):
    return codes.astype(jnp.int32).astype(jnp.float32)


def row_scales(tile):
    return jnp.exp2(as_float(tile)[0:1] * 0.125 - 15.0)


def level_tile(level):
    return jnp.broadcast_to(to_row(level), (TILE, GROUP)).astype(jnp.int32).astype(jnp.int16)


def prepare_kernel(grad_ref, ids_ref, lengths_ref, out_ref, grads, ids_buf, lengths_buf, outs, in_sems, out_sems):
    parts, block = grads.shape[0], grads.shape[2]
    samples = grads.shape[1]
    small = (
        pltpu.make_async_copy(lengths_ref, lengths_buf, in_sems.at[parts]),
        pltpu.make_async_copy(ids_ref, ids_buf, in_sems.at[parts + 1]),
    )
    large = [
        pltpu.make_async_copy(grad_ref.at[:, pl.ds(part * block, block), :], grads.at[part], in_sems.at[part])
        for part in range(parts)
    ]
    for copy in small:
        copy.start()
    for copy in large:
        copy.start()
    for copy in small:
        copy.wait()
    ids = ids_buf[...]
    position = lax.broadcasted_iota(jnp.int32, ids.shape, 1)
    code = jnp.where(position < lengths_buf[...][:, None, :], (GROUP + (ids & (GROUP - 1))) << (ids >> 7), 0)
    outs[:, samples:, :] = code.astype(jnp.float32).astype(jnp.bfloat16)
    back = []
    for part in range(parts):
        rows = pl.ds(part * block, block)
        large[part].wait()
        outs[rows, 0:samples, :] = jnp.swapaxes(grads[part], 0, 1)
        back.append(pltpu.make_async_copy(outs.at[rows], out_ref.at[rows], out_sems.at[part]))
        back[part].start()
    for copy in back:
        copy.wait()


def prepare(grad, ids, lengths, parts=4):
    samples, features, width = grad.shape
    slots = ids.shape[1]
    shape = (features, samples + slots, width)
    return pl.pallas_call(
        prepare_kernel,
        in_specs=[pl.BlockSpec(memory_space=pl.ANY)] * 3,
        out_specs=pl.BlockSpec(memory_space=pl.ANY),
        out_shape=jax.ShapeDtypeStruct(shape, jnp.bfloat16),
        scratch_shapes=[
            pltpu.VMEM((parts, samples, features // parts, width), jnp.bfloat16),
            pltpu.VMEM(ids.shape, jnp.int32),
            pltpu.VMEM(lengths.shape, jnp.int32),
            pltpu.VMEM(shape, jnp.bfloat16),
            pltpu.SemaphoreType.DMA((parts + 2,)),
            pltpu.SemaphoreType.DMA((parts,)),
        ],
        compiler_params=pltpu.CompilerParams(vmem_limit_bytes=60 << 20),
        cost_estimate=pl.CostEstimate(flops=0, bytes_accessed=5 << 20, transcendentals=0),
        name="prepare",
    )(grad, ids, lengths)


def hot_kernel(x_ref, ids_ref, out_ref, *, blocks):
    step = pl.program_id(0)

    @pl.when(step == 0)
    def _():
        out_ref[...] = jnp.zeros_like(out_ref)

    bags, values = [], []
    for block in range(blocks):
        ids = ids_ref[block]
        shift = lax.shift_right_logical(ids, 6) * 2
        bags.append((ids & (HALF - 1), lax.shift_left(jnp.ones_like(ids), shift)))
        values.append(x_ref[block, 0:GROUP, :])
    out_ref[...] += block_sum(bags, values)

    @pl.when(step == pl.num_programs(0) - 1)
    def _():
        for field in range(1, FIELDS - 1):
            out_ref[field * GROUP : (field + 1) * GROUP, :] *= field_scale(field)


def hot_sum(rows, ids, blocks=32):
    count, height, width = rows.shape
    return pl.pallas_call(
        functools.partial(hot_kernel, blocks=blocks),
        grid=(count // blocks,),
        in_specs=[
            pl.BlockSpec((blocks, height, width), lambda i: (i, 0, 0)),
            pl.BlockSpec((blocks, ids.shape[1], GROUP), lambda i: (i, 0, 0)),
        ],
        out_specs=pl.BlockSpec((V, width), lambda i: (0, 0)),
        out_shape=jax.ShapeDtypeStruct((V, width), jnp.float32),
        compiler_params=PARAMS,
        cost_estimate=pl.CostEstimate(flops=2 * V * count * GROUP * width, bytes_accessed=3 << 20, transcendentals=0),
        name="hot_sum",
    )(rows, ids)


def cold_kernel(x_ref, out_ref, rows_ref, total_ref, sems, *, blocks):
    parts = x_ref.shape[0] // blocks

    def copy(part):
        at = pl.ds(part * blocks, blocks)
        return pltpu.make_async_copy(x_ref.at[at], rows_ref.at[at], sems.at[part])

    for part in range(parts):
        copy(part).start()
    total_ref[...] = jnp.zeros_like(total_ref)

    def add(part, carry):
        copy(part).wait()
        bags, values = [], []
        for block in range(blocks):
            at = part * blocks + block
            bags.append(decode_ids(rows_ref[at, GROUP : GROUP + 8, :].astype(jnp.float32)))
            values.append(rows_ref[at, 0:GROUP, :])
        total_ref[...] += block_sum(bags, values)
        return carry

    lax.fori_loop(0, parts, add, 0)
    for field in range(FIELDS):
        rows = total_ref[field * GROUP : (field + 1) * GROUP, :] * field_scale(field)
        codes, level = quantized(rows)
        out_ref[field, 0:GROUP, :] = codes
        out_ref[field, GROUP:, :] = level_tile(level)


def cold_sum(rows, blocks=16):
    count, height, width = rows.shape
    return pl.pallas_call(
        functools.partial(cold_kernel, blocks=blocks),
        in_specs=[pl.BlockSpec(memory_space=pl.ANY)],
        out_specs=pl.BlockSpec(memory_space=pltpu.VMEM),
        out_shape=jax.ShapeDtypeStruct((FIELDS, GROUP + TILE, width), jnp.int16),
        scratch_shapes=[
            pltpu.VMEM(rows.shape, rows.dtype),
            pltpu.VMEM((V, width), jnp.float32),
            pltpu.SemaphoreType.DMA((count // blocks,)),
        ],
        compiler_params=PARAMS,
        cost_estimate=pl.CostEstimate(flops=10 * V * count * GROUP * width, bytes_accessed=3 << 20, transcendentals=0),
        name="cold_sum",
    )(rows)


def whole(body, out_shape, name, *operands):
    return pl.pallas_call(body, out_shape=out_shape, compiler_params=PARAMS, name=name)(*operands)


def stored_everywhere(rows, out_ref):
    codes, level = quantized_in_row(rows)
    tile = row_tile(level)
    for peer in range(FIELDS):
        out_ref[peer, 0:GROUP, :] = codes
        out_ref[peer, GROUP:, :] = tile


def peer_sum(pieces_ref):
    total = None
    for peer in range(FIELDS):
        piece = as_float(pieces_ref[peer, 0:GROUP, :]) * to_column(row_scales(pieces_ref[peer, GROUP:, :]))
        total = piece if total is None else total + piece
    return total


def spread(rows_ref, out_ref):
    stored_everywhere(rows_ref[...], out_ref)


def line_total(pieces_ref, out_ref):
    codes, level = quantized_in_row(peer_sum(pieces_ref))
    out_ref[0:GROUP, :] = codes
    out_ref[GROUP:, :] = row_tile(level)


def replica_total(pieces_ref, out_ref):
    stored_everywhere(peer_sum(pieces_ref), out_ref)


def update(codes_ref, table_ref, accum_ref, new_table_ref, new_accum_ref):
    for group in range(FIELDS):
        rows, one = slice(group * GROUP, (group + 1) * GROUP), slice(group, group + 1)
        codes = as_float(codes_ref[group, 0:GROUP, :])
        scales = row_scales(codes_ref[group, GROUP:, :])
        squares = to_row(jnp.sum(codes * codes, axis=1, keepdims=True))
        fresh = accum_ref[one, :] + squares * scales * scales * (1.0 / GROUP)
        step = to_column(scales * (learning_rate / (jnp.sqrt(fresh) + epsilon)))
        new_accum_ref[one, :] = fresh
        new_table_ref[rows, :] = table_ref[rows, :] - codes * step


def updated(name, codes, table, accum):
    shapes = (
        jax.ShapeDtypeStruct(table.shape, jnp.float32),
        jax.ShapeDtypeStruct((FIELDS, GROUP), jnp.float32),
    )
    new_table, new_accum = whole(update, shapes, name, codes, table, accum.reshape(FIELDS, GROUP))
    return new_table, new_accum.reshape(V)


def halve(rows, axis, mask, mine):
    half = rows.shape[0] // 2
    pairs = [(i, i ^ mask) for i in range(lax.axis_size(axis))]
    got = lax.ppermute(lax.dynamic_slice_in_dim(rows, (1 - mine) * half, half), axis, pairs)
    return lax.dynamic_slice_in_dim(rows, mine * half, half) + got


def double(rows, axis, mask, mine):
    got = lax.ppermute(rows, axis, [(i, i ^ mask) for i in range(lax.axis_size(axis))])
    return jnp.where(mine == 0, jnp.concatenate([rows, got], 0), jnp.concatenate([got, rows], 0))


def per_device(pooled_grad, cold_ids, lengths, hot_ids, table, accum, hot_table, hot_accum):
    lines = [[y * 8 + inner for y in range(8)] for inner in range(8)]
    coded = jax.ShapeDtypeStruct((FIELDS, GROUP + TILE, GROUP), jnp.int16)
    rows = prepare(pooled_grad, jnp.transpose(cold_ids, (1, 2, 0)), jnp.transpose(lengths, (1, 0)))
    moved = lax.all_to_all(rows, "shard", split_axis=0, concat_axis=0, tiled=True)
    hot = hot_sum(rows, jnp.transpose(hot_ids, (1, 2, 0)))
    me = lax.axis_index("shard")
    core, low, high = me & 1, (me >> 1) & 1, (me >> 2) & 1
    rounds = ((1, core), (6, high), (2, low ^ high))
    for mask, mine in rounds:
        hot = halve(hot, "shard", mask, mine)
    for bit in (1, 2, 4):
        hot = hot + lax.ppermute(hot, "rep", [(i, i ^ bit) for i in range(FIELDS)])
    hot = whole(spread, coded, "spread", hot)
    moved, hot = lax.optimization_barrier((moved, hot))
    hot = lax.all_to_all(hot, "shard", split_axis=0, concat_axis=0, axis_index_groups=lines, tiled=True)
    pieces = cold_sum(moved)
    pieces, hot = lax.optimization_barrier((pieces, hot))
    shared = lax.all_to_all(pieces, "rep", split_axis=0, concat_axis=0, tiled=True)
    hot = whole(line_total, jax.ShapeDtypeStruct(coded.shape[1:], jnp.int16), "line_total", hot)
    payload = whole(replica_total, coded, "replica_total", shared)
    hot = double(hot, "shard", *rounds[2])
    codes = lax.all_to_all(payload, "rep", split_axis=0, concat_axis=0, tiled=True)
    for mask, mine in rounds[1::-1]:
        hot = double(hot, "shard", mask, mine)
    new_hot_table, new_hot_accum = updated("hot_update", hot.reshape(coded.shape), hot_table, hot_accum)
    new_table, new_accum = updated("cold_update", codes, table, accum)
    return (new_table, new_accum, new_hot_table, new_hot_accum)


def solution(mesh):
    in_specs = (
        P(("shard", "rep"), None, None),
        P(("shard", "rep"), None, None),
        P(("shard", "rep"), None),
        P(("shard", "rep"), None, None),
        P("shard", None),
        P("shard"),
        P(),
        P(),
    )
    out_specs = (P("shard", None), P("shard"), P(), P())
    return jax.shard_map(
        per_device, mesh=mesh, in_specs=in_specs, out_specs=out_specs, check_vma=False
    )
```

```python
import functools

import jax
import jax.numpy as jnp
from jax import lax
from jax.experimental import pallas as pl
from jax.experimental.pallas import tpu as pltpu
from jax.sharding import PartitionSpec as P

V = 1024
GROUP = 128
HALF = 64
FIELDS = 8
BITS = 4
TILE = 8
PAIRS = 0x33333333

learning_rate = 0.5
epsilon = 1e-06

PARAMS = pltpu.CompilerParams(vmem_limit_bytes=40 << 20)


def decode_ids(code):
    key = jnp.zeros(code.shape, jnp.float32)
    unit = jnp.zeros(code.shape, jnp.int32)
    for field in range(FIELDS):
        reached = code >= float(GROUP * 2**field)
        key = jnp.where(reached, code * 2.0**-field - float(GROUP), key)
        unit = jnp.where(reached, 1 << (BITS * field), unit)
    upper = key >= float(HALF)
    key = jnp.where(upper, key - float(HALF), key)
    return key.astype(jnp.int32), jnp.where(upper, unit * 4, unit)


def packed_counts(key, unit):
    rows = lax.broadcasted_iota(jnp.int32, (HALF, key.shape[1]), 0)
    even = odd = None
    for first in range(0, key.shape[0], 3):
        total = None
        for slot in range(first, min(first + 3, key.shape[0])):
            term = jnp.where(rows == key[slot : slot + 1], unit[slot : slot + 1], 0)
            total = term if total is None else total + term
        low, high = total & PAIRS, lax.shift_right_logical(total, 2) & PAIRS
        even = low if even is None else even + low
        odd = high if odd is None else odd + high
    return even, odd


def unpacked_counts(even, odd):
    groups = []
    for field in range(FIELDS):
        for packed in (even, odd):
            if field == FIELDS - 1:
                part = lax.shift_right_logical(packed, BITS * field)
            else:
                part = packed & (((1 << BITS) - 1) << (BITS * field))
            groups.append(part.astype(jnp.float32).astype(jnp.bfloat16))
    return jnp.concatenate(groups, 0)


def field_scale(field):
    return 2.0 ** (-BITS * field) if field < FIELDS - 1 else 1.0


def block_sum(bags, values):
    total = None
    for bag, rows in zip(bags, values):
        product = jnp.dot(unpacked_counts(*packed_counts(*bag)), rows, preferred_element_type=jnp.float32)
        total = product if total is None else total + product
    return total


def diagonal(rows):
    shape = (rows, GROUP)
    return lax.broadcasted_iota(jnp.int32, shape, 0) == lax.broadcasted_iota(jnp.int32, shape, 1)


def to_row(column):
    return jnp.sum(jnp.where(diagonal(column.shape[0]), column, 0.0), axis=0, keepdims=True)


def to_column(row, rows=GROUP):
    return jnp.sum(jnp.where(diagonal(rows), row, 0.0), axis=1, keepdims=True)


def quantized(x):
    top = jnp.maximum(jnp.max(jnp.abs(x), axis=1, keepdims=True), 1e-30)
    level = jnp.ceil(8.0 * jnp.log2(top) + 0.05)
    return jnp.round(x * jnp.exp2(15.0 - level * 0.125)).astype(jnp.int32).astype(jnp.int16), level


def as_float(codes):
    return codes.astype(jnp.int32).astype(jnp.float32)


def row_scales(tile):
    return jnp.exp2(as_float(tile)[0:1] * 0.125 - 15.0)


def level_tile(level):
    return jnp.broadcast_to(to_row(level), (TILE, GROUP)).astype(jnp.int32).astype(jnp.int16)


def prepare_kernel(grad_ref, ids_ref, lengths_ref, out_ref, grads, ids_buf, lengths_buf, outs, in_sems, out_sems):
    parts, block = grads.shape[0], grads.shape[2]
    samples = grads.shape[1]
    small = (
        pltpu.make_async_copy(lengths_ref, lengths_buf, in_sems.at[parts]),
        pltpu.make_async_copy(ids_ref, ids_buf, in_sems.at[parts + 1]),
    )
    large = [
        pltpu.make_async_copy(grad_ref.at[:, pl.ds(part * block, block), :], grads.at[part], in_sems.at[part])
        for part in range(parts)
    ]
    for copy in small:
        copy.start()
    for copy in large:
        copy.start()
    for copy in small:
        copy.wait()
    ids = ids_buf[...]
    position = lax.broadcasted_iota(jnp.int32, ids.shape, 1)
    code = jnp.where(position < lengths_buf[...][:, None, :], (GROUP + (ids & (GROUP - 1))) << (ids >> 7), 0)
    outs[:, samples:, :] = code.astype(jnp.float32).astype(jnp.bfloat16)
    back = []
    for part in range(parts):
        rows = pl.ds(part * block, block)
        large[part].wait()
        outs[rows, 0:samples, :] = jnp.swapaxes(grads[part], 0, 1)
        back.append(pltpu.make_async_copy(outs.at[rows], out_ref.at[rows], out_sems.at[part]))
        back[part].start()
    for copy in back:
        copy.wait()


def prepare(grad, ids, lengths, parts=4):
    samples, features, width = grad.shape
    slots = ids.shape[1]
    shape = (features, samples + slots, width)
    return pl.pallas_call(
        prepare_kernel,
        in_specs=[pl.BlockSpec(memory_space=pl.ANY)] * 3,
        out_specs=pl.BlockSpec(memory_space=pl.ANY),
        out_shape=jax.ShapeDtypeStruct(shape, jnp.bfloat16),
        scratch_shapes=[
            pltpu.VMEM((parts, samples, features // parts, width), jnp.bfloat16),
            pltpu.VMEM(ids.shape, jnp.int32),
            pltpu.VMEM(lengths.shape, jnp.int32),
            pltpu.VMEM(shape, jnp.bfloat16),
            pltpu.SemaphoreType.DMA((parts + 2,)),
            pltpu.SemaphoreType.DMA((parts,)),
        ],
        compiler_params=pltpu.CompilerParams(vmem_limit_bytes=60 << 20),
        cost_estimate=pl.CostEstimate(flops=0, bytes_accessed=5 << 20, transcendentals=0),
        name="prepare",
    )(grad, ids, lengths)


def hot_kernel(x_ref, ids_ref, out_ref, *, blocks):
    step = pl.program_id(0)

    @pl.when(step == 0)
    def _():
        out_ref[...] = jnp.zeros_like(out_ref)

    bags, values = [], []
    for block in range(blocks):
        ids = ids_ref[block]
        shift = lax.shift_right_logical(ids, 6) * 2
        bags.append((ids & (HALF - 1), lax.shift_left(jnp.ones_like(ids), shift)))
        values.append(x_ref[block, 0:GROUP, :])
    out_ref[...] += block_sum(bags, values)

    @pl.when(step == pl.num_programs(0) - 1)
    def _():
        for field in range(1, FIELDS - 1):
            out_ref[field * GROUP : (field + 1) * GROUP, :] *= field_scale(field)


def hot_sum(rows, ids, blocks=32):
    count, height, width = rows.shape
    return pl.pallas_call(
        functools.partial(hot_kernel, blocks=blocks),
        grid=(count // blocks,),
        in_specs=[
            pl.BlockSpec((blocks, height, width), lambda i: (i, 0, 0)),
            pl.BlockSpec((blocks, ids.shape[1], GROUP), lambda i: (i, 0, 0)),
        ],
        out_specs=pl.BlockSpec((V, width), lambda i: (0, 0)),
        out_shape=jax.ShapeDtypeStruct((V, width), jnp.float32),
        compiler_params=PARAMS,
        cost_estimate=pl.CostEstimate(flops=2 * V * count * GROUP * width, bytes_accessed=3 << 20, transcendentals=0),
        name="hot_sum",
    )(rows, ids)


def cold_kernel(x_ref, out_ref, rows_ref, total_ref, sems, *, blocks):
    parts = x_ref.shape[0] // blocks

    def copy(part):
        at = pl.ds(part * blocks, blocks)
        return pltpu.make_async_copy(x_ref.at[at], rows_ref.at[at], sems.at[part])

    for part in range(parts):
        copy(part).start()
    total_ref[...] = jnp.zeros_like(total_ref)

    def add(part, carry):
        copy(part).wait()
        bags, values = [], []
        for block in range(blocks):
            at = part * blocks + block
            bags.append(decode_ids(rows_ref[at, GROUP : GROUP + 8, :].astype(jnp.float32)))
            values.append(rows_ref[at, 0:GROUP, :])
        total_ref[...] += block_sum(bags, values)
        return carry

    lax.fori_loop(0, parts, add, 0)
    for field in range(FIELDS):
        rows = total_ref[field * GROUP : (field + 1) * GROUP, :] * field_scale(field)
        codes, level = quantized(rows)
        out_ref[field, 0:GROUP, :] = codes
        out_ref[field, GROUP:, :] = level_tile(level)


def cold_sum(rows, blocks=32):
    count, height, width = rows.shape
    return pl.pallas_call(
        functools.partial(cold_kernel, blocks=blocks),
        in_specs=[pl.BlockSpec(memory_space=pl.ANY)],
        out_specs=pl.BlockSpec(memory_space=pltpu.VMEM),
        out_shape=jax.ShapeDtypeStruct((FIELDS, GROUP + TILE, width), jnp.int16),
        scratch_shapes=[
            pltpu.VMEM(rows.shape, rows.dtype),
            pltpu.VMEM((V, width), jnp.float32),
            pltpu.SemaphoreType.DMA((count // blocks,)),
        ],
        compiler_params=PARAMS,
        cost_estimate=pl.CostEstimate(flops=10 * V * count * GROUP * width, bytes_accessed=3 << 20, transcendentals=0),
        name="cold_sum",
    )(rows)


def whole(body, out_shape, name, *operands):
    return pl.pallas_call(body, out_shape=out_shape, compiler_params=PARAMS, name=name)(*operands)


def stored_everywhere(rows, out_ref):
    codes, level = quantized(rows)
    tile = level_tile(level)
    for peer in range(FIELDS):
        out_ref[peer, 0:GROUP, :] = codes
        out_ref[peer, GROUP:, :] = tile


def peer_sum(pieces_ref):
    total = None
    for peer in range(FIELDS):
        piece = as_float(pieces_ref[peer, 0:GROUP, :]) * to_column(row_scales(pieces_ref[peer, GROUP:, :]))
        total = piece if total is None else total + piece
    return total


def spread(rows_ref, out_ref):
    stored_everywhere(rows_ref[...], out_ref)


def line_total(pieces_ref, out_ref):
    codes, level = quantized(peer_sum(pieces_ref))
    out_ref[0:GROUP, :] = codes
    out_ref[GROUP:, :] = level_tile(level)


def replica_total(pieces_ref, out_ref):
    stored_everywhere(peer_sum(pieces_ref), out_ref)


def update(codes_ref, table_ref, accum_ref, new_table_ref, new_accum_ref):
    for group in range(FIELDS):
        rows, one = slice(group * GROUP, (group + 1) * GROUP), slice(group, group + 1)
        codes = as_float(codes_ref[group, 0:GROUP, :])
        scales = row_scales(codes_ref[group, GROUP:, :])
        squares = to_row(jnp.sum(codes * codes, axis=1, keepdims=True))
        fresh = accum_ref[one, :] + squares * scales * scales * (1.0 / GROUP)
        step = to_column(scales * (learning_rate / (jnp.sqrt(fresh) + epsilon)))
        new_accum_ref[one, :] = fresh
        new_table_ref[rows, :] = table_ref[rows, :] - codes * step


def updated(name, codes, table, accum):
    shapes = (
        jax.ShapeDtypeStruct(table.shape, jnp.float32),
        jax.ShapeDtypeStruct((FIELDS, GROUP), jnp.float32),
    )
    new_table, new_accum = whole(update, shapes, name, codes, table, accum.reshape(FIELDS, GROUP))
    return new_table, new_accum.reshape(V)


def halve(rows, axis, mask, mine):
    half = rows.shape[0] // 2
    pairs = [(i, i ^ mask) for i in range(lax.axis_size(axis))]
    got = lax.ppermute(lax.dynamic_slice_in_dim(rows, (1 - mine) * half, half), axis, pairs)
    return lax.dynamic_slice_in_dim(rows, mine * half, half) + got


def double(rows, axis, mask, mine):
    got = lax.ppermute(rows, axis, [(i, i ^ mask) for i in range(lax.axis_size(axis))])
    return jnp.where(mine == 0, jnp.concatenate([rows, got], 0), jnp.concatenate([got, rows], 0))


def per_device(pooled_grad, cold_ids, lengths, hot_ids, table, accum, hot_table, hot_accum):
    lines = [[y * 8 + inner for y in range(8)] for inner in range(8)]
    coded = jax.ShapeDtypeStruct((FIELDS, GROUP + TILE, GROUP), jnp.int16)
    rows = prepare(pooled_grad, jnp.transpose(cold_ids, (1, 2, 0)), jnp.transpose(lengths, (1, 0)))
    moved = lax.all_to_all(rows, "shard", split_axis=0, concat_axis=0, tiled=True)
    hot = hot_sum(rows, jnp.transpose(hot_ids, (1, 2, 0)))
    me = lax.axis_index("shard")
    core, low, high = me & 1, (me >> 1) & 1, (me >> 2) & 1
    rounds = ((1, core), (6, high), (2, low ^ high))
    for mask, mine in rounds:
        hot = halve(hot, "shard", mask, mine)
    for bit in (1, 2, 4):
        hot = hot + lax.ppermute(hot, "rep", [(i, i ^ bit) for i in range(FIELDS)])
    hot = whole(spread, coded, "spread", hot)
    moved, hot = lax.optimization_barrier((moved, hot))
    hot = lax.all_to_all(hot, "shard", split_axis=0, concat_axis=0, axis_index_groups=lines, tiled=True)
    pieces = cold_sum(moved)
    pieces, hot = lax.optimization_barrier((pieces, hot))
    shared = lax.all_to_all(pieces, "rep", split_axis=0, concat_axis=0, tiled=True)
    hot = whole(line_total, jax.ShapeDtypeStruct(coded.shape[1:], jnp.int16), "line_total", hot)
    payload = whole(replica_total, coded, "replica_total", shared)
    hot = double(hot, "shard", *rounds[2])
    codes = lax.all_to_all(payload, "rep", split_axis=0, concat_axis=0, tiled=True)
    for mask, mine in rounds[1::-1]:
        hot = double(hot, "shard", mask, mine)
    new_hot_table, new_hot_accum = updated("hot_update", hot.reshape(coded.shape), hot_table, hot_accum)
    new_table, new_accum = updated("cold_update", codes, table, accum)
    return (new_table, new_accum, new_hot_table, new_hot_accum)


def solution(mesh):
    in_specs = (
        P(("shard", "rep"), None, None),
        P(("shard", "rep"), None, None),
        P(("shard", "rep"), None),
        P(("shard", "rep"), None, None),
        P("shard", None),
        P("shard"),
        P(),
        P(),
    )
    out_specs = (P("shard", None), P("shard"), P(), P())
    return jax.shard_map(
        per_device, mesh=mesh, in_specs=in_specs, out_specs=out_specs, check_vma=False
    )
```
